256 devices in a mesh: grp: 16 (over x, y_lo, core), blk: 16 (over y_hi, z).
Axes of the slice: x: 4, y: 4 (y_hi: 2, y_lo: 2; y = y_hi * 2 + y_lo), z: 8, core: 2. Of those that a mesh axis runs over, the one named last changes fastest.
Arguments:
- member_embed: float32 [16, 4096, 768], P('grp', 'blk'), may hold values from -64 to 64
- sizes: int32 [16], replicated, may hold values from 1 to 4096, 32768 in all
- order: int32 [16, 4096], P('grp', 'blk'), may hold values from 0 to 4095, each once within a row
- ref_embed: float32 [16, 8192, 768], P(None, ('grp', 'blk')), may hold values from -64 to 64
Outputs:
- log_total: float32 [16, 4096], P('grp', 'blk')
- neighbour: bfloat16 [16, 4096, 768], P('grp', 'blk')
The draws below stay inside these ranges and needn't reach their ends.
Inputs may be any that keep to these rules, and one draw needn't show every extreme that they name: Each cluster's row of order is a permutation of 0 to 4095.
All inputs are finite; a program needn't handle non-finite values.
Results may differ from the reference program's by a relative error of at most 0.0068.
Values may be sent and summed in bfloat16 or wider, within the bound.
A program may use at most 128 MiB of HBM per device.

```python
import math
import jax
import jax.numpy as jnp
import numpy as np
from jax import lax

D = 768
SCALE = 32
CLUSTERS = 16
MEMBERS = 4096
REFS = 8192


def geometry(key):
    first = jax.random.fold_in(jax.random.fold_in(key, 11), 0)
    column_scale = jnp.exp(jax.random.uniform(first, (CLUSTERS, 1, D)) * math.log(30.0))
    return column_scale


def scaled_rows(base, row_key, row_count, spread, column_scale):
    row_scale = jnp.exp(jax.random.uniform(row_key, (CLUSTERS, row_count, 1)) * math.log(spread))
    return jnp.clip(base * column_scale * row_scale, -64.0, 64.0)


def draw_member_embed(key, part):
    column_scale = geometry(key)
    key = jax.random.fold_in(key, 3)
    first, second = jax.random.split(key)
    base = jax.random.normal(first, (CLUSTERS, MEMBERS, D))
    return scaled_rows(base, second, MEMBERS, 10.0, column_scale)


def draw_ref_embed(key, part):
    column_scale = geometry(key)
    key = jax.random.fold_in(key, 5)
    first, second = jax.random.split(key)
    base = jax.random.normal(first, (CLUSTERS, REFS, D))
    return scaled_rows(base, second, REFS, 10.0, column_scale)


def split_up(amount, total, limit, lean):
    weights = [(1 << 20) // math.isqrt(grade ** lean) + 1 for grade in range(2, amount + 1)]
    rest, given = total - limit - (amount - 1), [1] * (amount - 1)
    while rest > 0:
        candidates = [i for i in range(amount - 1) if given[i] < limit]
        whole, budget = sum([weights[i] for i in candidates]), rest
        for i in candidates:
            extra = min(limit - given[i], max(1, budget * weights[i] // whole), rest)
            given[i] = given[i] + extra
            rest = rest - extra
    return np.array([limit] + given)


def uneven_parts(stream_key, amount, total, most, lean):
    if amount == 2:
        one = jax.random.randint(stream_key, (), max(1, total - most), min(most, total - 1) + 1)
        return jnp.stack([one, total - one])
    sizes = jnp.asarray(split_up(amount, total, most, lean), jnp.int32)
    twos = (amount - 1) // 2
    giver, sink = sizes[1:1 + 2 * twos:2], sizes[2:2 + 2 * twos:2]
    slack = jnp.minimum(giver - 1, most - sink)
    moved = jax.random.randint(jax.random.fold_in(stream_key, 1), (twos,), 0, 1 << 20) % (slack + 1)
    sizes = sizes.at[1:1 + 2 * twos:2].set(giver - moved).at[2:2 + 2 * twos:2].set(sink + moved)
    return sizes[jax.random.permutation(jax.random.fold_in(stream_key, 2), amount)]


def setup_inputs(seed: int = 0) -> dict:
    key_list = jax.random.split(jax.random.key(seed), 5)
    return {
        "member_embed": draw_member_embed(jax.random.fold_in(key_list[4], 71), 0),
        "sizes": uneven_parts(key_list[1], CLUSTERS, CLUSTERS * MEMBERS // 2, MEMBERS, 2).astype(jnp.int32),
        "order": jax.vmap(lambda own: jax.random.permutation(own, MEMBERS))(jax.random.split(key_list[2], CLUSTERS)).reshape((CLUSTERS, MEMBERS)).astype(jnp.int32),
        "ref_embed": draw_ref_embed(jax.random.fold_in(key_list[4], 71), 0),
    }


def unit_rows(values):
    mean_square = lax.optimization_barrier(jnp.mean(values * values, axis=-1, keepdims=True))
    return (values * lax.rsqrt(mean_square + 1e-06)).astype(jnp.bfloat16)

def inner_rows(left, right):
    return lax.dot_general(left, right, (((1,), (1,)), ((), ())), preferred_element_type=jnp.float32)

def reference(member_embed, sizes, order, ref_embed):
    members = unit_rows(member_embed)
    references = unit_rows(ref_embed)
    block_rows = 512 if MEMBERS % 512 == 0 else MEMBERS
    logit_scale = SCALE / D

    def one_cluster(packed):
        key_rows, ref_rows, key_order, live_count = packed
        live_rows = jnp.arange(MEMBERS, dtype=jnp.int32) < live_count
        key_ranks = jnp.where(live_rows, key_order, MEMBERS).astype(jnp.int32)

        def one_block(index):
            offset = (index * block_rows).astype(jnp.int32)
            queries = lax.dynamic_slice_in_dim(key_rows, offset, block_rows, 0)
            query_ranks = lax.dynamic_slice_in_dim(key_order, offset, block_rows, 0)
            member_logits = inner_rows(queries, key_rows)
            member_weight = jnp.where(key_ranks[None, :] < query_ranks[:, None], jnp.exp(member_logits * logit_scale - SCALE), 0.0)
            ref_weight = jnp.exp(inner_rows(queries, ref_rows) * logit_scale - SCALE)
            denominator = lax.optimization_barrier(jnp.sum(member_weight, axis=1)) + lax.optimization_barrier(jnp.sum(ref_weight, axis=1))
            weighted = jnp.dot(member_weight.astype(jnp.bfloat16), key_rows, preferred_element_type=jnp.float32)
            weighted = weighted + jnp.dot(ref_weight.astype(jnp.bfloat16), ref_rows, preferred_element_type=jnp.float32)
            return (denominator, weighted)
        denominators, weighted = lax.map(one_block, jnp.arange(MEMBERS // block_rows, dtype=jnp.int32))
        denominators = denominators.reshape(MEMBERS)
        weighted = weighted.reshape(MEMBERS, D)
        divisor = jnp.where(live_rows, denominators, 1.0)
        log_values = jnp.where(live_rows, SCALE + jnp.log(divisor), 0.0)
        mean_rows = jnp.where(live_rows[:, None], weighted / divisor[:, None], 0.0).astype(jnp.bfloat16)
        return (log_values, mean_rows)
    log_total, neighbour = lax.map(one_cluster, (members, references, order, sizes))
    return (log_total, neighbour)
```

```python
import functools
import math

import jax
import jax.numpy as jnp
from jax import lax
from jax.experimental import pallas as pl
from jax.experimental.pallas import tpu as pltpu
from jax.sharding import PartitionSpec as P

SCALE = 32
MESH = pl.DeviceIdType.MESH
LOG2E = math.log2(math.e)
STEPS = (0, 1, 7, 2, 6, 3, 5, 4)


def unit_rows(values):
    mean_square = jnp.mean(values * values, axis=-1, keepdims=True)
    return (values * lax.rsqrt(mean_square + 1e-06)).astype(jnp.bfloat16)


def device(x, y, z, core):
    return ((x * 2 + y % 2) * 2 + core, (y // 2) * 8 + z)


def lanes_to_rows(tile):
    wide = jnp.concatenate([tile] * 8, axis=0)
    row = lax.broadcasted_iota(jnp.int32, (64, 128), 0)
    lane = lax.broadcasted_iota(jnp.int32, (64, 128), 1)
    return jnp.sum(jnp.where(row == lane, wide, 0.0), axis=1, keepdims=True)


def rows_to_lanes(column):
    row = lax.broadcasted_iota(jnp.int32, (64, 128), 0)
    lane = lax.broadcasted_iota(jnp.int32, (64, 128), 1)
    spread = jnp.where(row == lane % 64, jnp.broadcast_to(column, (64, 128)), 0.0)
    return jnp.broadcast_to(jnp.sum(spread, axis=0, keepdims=True), (8, 128))


def slot_position(delta):
    return delta + delta // 2 - 2 * (delta // 3)


def kernel(
    member_hbm, sizes_ref, order_ref, ref_hbm, log_ref, mean_ref,
    member_in, ref_in, home_rows, home_rank, ref_unit, query, rank, key_member, rank_partner, ref_other, key_ref,
    part_sum, part_total, mix_send, mix_recv, tot_send, tot_recv, own_mix, own_tot,
    x_send, x_recv, xt_send, xt_recv, done_rows, done_log, home_log,
    load_sem, s_a, r_a, s_x, r_x, s_c, r_c, s_y, r_y, s_z, r_z, s_ry, r_ry,
    s_m, r_m, s_t, r_t, s_h, r_h,
):
    g = lax.axis_index("grp")
    b = lax.axis_index("blk")
    x, y, z, core = g // 4, (b // 8) * 2 + (g // 2) % 2, b % 8, g % 2
    parity = y % 2
    other = 1 - core
    home_z = 2 * x + core
    work_x, work_core = z // 2, z % 2
    is_self = home_z == z
    work_group = (work_x * 2 + parity) * 2 + work_core

    def source_z(position):
        return 2 * ((z // 2 + slot_position(position)) % 4) + core

    load_members = pltpu.make_async_copy(member_hbm.at[0], member_in, load_sem.at[0])
    load_refs = pltpu.make_async_copy(ref_hbm, ref_in, load_sem.at[1])
    load_members.start()
    load_refs.start()

    barrier = pltpu.get_barrier_semaphore()

    def greet(target):
        pl.semaphore_signal(barrier, inc=1, device_id=target, device_id_type=MESH)

    for step in (1, 2, 3):
        greet(device((x + step) % 4, y, z, core))
        greet(device(x, (y + step) % 4, z, core))
    for step in range(1, 8):
        greet(device(x, y, (z + step) % 8, core))
    greet(device(x, y, z, other))
    for position in range(4):
        from_z = source_z(position)

        @pl.when(jnp.logical_not(jnp.logical_and(is_self, from_z == z)))
        def _():
            greet(device(work_x, y, from_z, work_core))

    for quarter in range(4):

        @pl.when(jnp.logical_not(jnp.logical_and(is_self, x == quarter)))
        def _():
            greet(device(quarter, y, home_z, z % 2))

    load_members.wait()
    home_rows[...] = unit_rows(member_in[...])
    live_count = sizes_ref[g]
    slot = lax.broadcasted_iota(jnp.int32, (1, 256), 1) + b * 256
    ranks = jnp.where(slot < live_count, order_ref[...], 4096).astype(jnp.float32)
    for quarter in range(4):
        piece = ranks[:, 64 * quarter : 64 * quarter + 64]
        home_rank[quarter] = jnp.broadcast_to(jnp.concatenate([piece, piece], axis=1), (8, 128))

    pl.semaphore_wait(barrier, 22 - 2 * is_self.astype(jnp.int32))

    sent = []

    def send(src, dst, send_sem, recv_sem, target):
        copy = pltpu.make_async_remote_copy(
            src_ref=src, dst_ref=dst, send_sem=send_sem, recv_sem=recv_sem, device_id=target, device_id_type=MESH
        )
        copy.start()
        sent.append(copy)
        return copy

    def landed(dst, sem):
        pltpu.make_async_copy(dst, dst, sem).wait()

    here = slot_position((z // 2 - home_z // 2 + 4) % 4)
    row_owner = z % 2 * 4
    first = []
    for quarter in range(4):
        pairs = (
            (home_rows.at[pl.ds(64 * quarter, 64)], query.at[here, row_owner + quarter], 0),
            (home_rank.at[quarter], rank.at[here, row_owner + quarter], 1),
        )
        target = device(quarter, y, home_z, z % 2)
        mine = jnp.logical_and(is_self, x == quarter)
        for src, dst, kind in pairs:
            remote = pltpu.make_async_remote_copy(
                src_ref=src, dst_ref=dst, send_sem=s_a.at[kind, quarter], recv_sem=r_a.at[kind, here],
                device_id=target, device_id_type=MESH,
            )
            local = pltpu.make_async_copy(src, dst, r_a.at[kind, here])
            first.append((mine, remote))

            @pl.when(mine)
            def _():
                local.start()

            @pl.when(jnp.logical_not(mine))
            def _():
                remote.start()

    load_refs.wait()
    for group in range(4):
        ref_unit[pl.ds(4 * group, 4)] = unit_rows(ref_in[pl.ds(4 * group, 4)])

    def ref_index(to_z, side):
        return (to_z // 2) * 4 + side * 2 + to_z % 2

    key_ref[0, 0] = ref_unit[ref_index(z, parity)]
    ref_other[0] = ref_unit[ref_index(z, 1 - parity)]
    for i in range(1, 8):
        to_z = (z + 8 - STEPS[i]) % 8
        target = device(x, y, to_z, core)
        send(ref_unit.at[ref_index(to_z, parity)], key_ref.at[i, 0], s_z.at[0, i], r_z.at[0, i], target)
        send(ref_unit.at[ref_index(to_z, 1 - parity)], ref_other.at[i], s_z.at[1, i], r_z.at[1, i], target)

    opposite = device(x, (y + 2) % 4, z, core)
    above = device(x, (y + 1) % 4, z, core)
    below = device(x, (y + 3) % 4, z, core)

    def pass_refs(i):
        if i:
            landed(key_ref.at[i, 0], r_z.at[0, i])
            landed(ref_other.at[i], r_z.at[1, i])
        send(key_ref.at[i, 0], key_ref.at[i, 1], s_ry.at[0, i], r_ry.at[0, i], opposite)
        send(ref_other.at[i], key_ref.at[i, 2], s_ry.at[1, i], r_ry.at[1, i], above)
        send(ref_other.at[i], key_ref.at[i, 3], s_ry.at[2, i], r_ry.at[2, i], below)

    pass_refs(0)

    me = core * 4 + x

    def pass_queries(t):
        landed(query.at[t, me], r_a.at[0, t])
        landed(rank.at[t, me], r_a.at[1, t])
        for step in (2, 1, 3):
            target = device((x + step) % 4, y, z, core)
            send(query.at[t, me], query.at[t, me], s_x.at[0, step - 1, t], r_x.at[0, step - 1, t], target)
            send(rank.at[t, me], rank.at[t, me], s_x.at[1, step - 1, t], r_x.at[1, step - 1, t], target)
        send(query.at[t, me], key_member.at[1, t], s_y.at[0, t], r_y.at[0, t], opposite)
        send(rank.at[t, me], rank_partner.at[t], s_y.at[1, t], r_y.at[1, t], opposite)
        key_member[0, t] = query[t, me]

    sibling = device(x, y, z, other)
    my_half, other_half = pl.ds(core * 4, 4), pl.ds(other * 4, 4)

    def share_queries(t):
        for step in (1, 3, 2):
            from_x = core * 4 + (x + 4 - step) % 4
            landed(query.at[t, from_x], r_x.at[0, step - 1, t])
            landed(rank.at[t, from_x], r_x.at[1, step - 1, t])
        send(query.at[t, my_half], query.at[t, my_half], s_c.at[0, t], r_c.at[0, t], sibling)
        send(rank.at[t, my_half], rank.at[t, my_half], s_c.at[1, t], r_c.at[1, t], sibling)

    for t in range(4):
        pass_queries(t)
    pass_refs(1)
    pass_refs(2)
    share_queries(0)
    pass_refs(3)
    pass_refs(4)
    share_queries(1)
    pass_refs(5)
    pass_refs(6)
    share_queries(2)
    pass_refs(7)
    share_queries(3)

    for t in range(4):
        landed(key_member.at[1, t], r_y.at[0, t])
        landed(rank_partner.at[t], r_y.at[1, t])
        landed(query.at[t, other_half], r_c.at[0, t])
        landed(rank.at[t, other_half], r_c.at[1, t])
    for i in range(8):
        for side in range(3):
            landed(key_ref.at[i, side + 1], r_ry.at[side, i])

    low = lax.broadcasted_iota(jnp.int32, (8, 128), 1) < 64
    key_rank = jnp.concatenate(
        [
            jnp.where(low, rank[0, me], rank[1, me]),
            jnp.where(low, rank[2, me], rank[3, me]),
            jnp.where(low, rank_partner[0], rank_partner[1]),
            jnp.where(low, rank_partner[2], rank_partner[3]),
        ],
        axis=1,
    )[0:1]

    def weigh(rows, keys):
        logits = lax.dot_general(rows, keys, (((1,), (1,)), ((), ())), preferred_element_type=jnp.float32)
        return jnp.exp2(logits * (SCALE / 768 * LOG2E) - SCALE * LOG2E)

    def compute(t):
        rows = query[t].reshape(512, 768)
        row_rank = jnp.concatenate([lanes_to_rows(rank[t, owner]) for owner in range(8)], axis=0)
        keys = key_member[...].reshape(512, 768)
        weight = jnp.where(key_rank < row_rank, weigh(rows, keys), 0.0)
        total = jnp.sum(weight, axis=1, keepdims=True)
        mixed = jnp.dot(weight.astype(jnp.bfloat16), keys, preferred_element_type=jnp.float32)
        for half in range(2):
            keys = key_ref[pl.ds(4 * half, 4)].reshape(512, 768)
            weight = weigh(rows, keys)
            total = total + jnp.sum(weight, axis=1, keepdims=True)
            mixed = mixed + jnp.dot(weight.astype(jnp.bfloat16), keys, preferred_element_type=jnp.float32)
        part_sum[t] = mixed.reshape(8, 64, 768)
        for owner in range(8):
            part_total[t, owner] = rows_to_lanes(total[64 * owner : 64 * owner + 64])
        mix_send[t] = part_sum[t, other_half].astype(jnp.bfloat16)
        tot_send[t] = part_total[t, other_half]
        send(mix_send.at[t], mix_recv.at[t], s_m.at[0, t], r_m.at[0, t], sibling)
        send(tot_send.at[t], tot_recv.at[t], s_m.at[1, t], r_m.at[1, t], sibling)

    def to_owner(t):
        landed(mix_recv.at[t], r_m.at[0, t])
        landed(tot_recv.at[t], r_m.at[1, t])
        mixed = part_sum[t, my_half] + mix_recv[t].astype(jnp.float32)
        total = part_total[t, my_half] + tot_recv[t]
        part_sum[t, my_half] = mixed
        part_total[t, my_half] = total
        x_send[t] = mixed.astype(jnp.bfloat16)
        xt_send[t] = total
        for step in (2, 1, 3):
            to_x = (x + step) % 4
            target = device(to_x, y, z, core)
            send(x_send.at[t, to_x], x_recv.at[t, step - 1], s_t.at[0, step - 1, t], r_t.at[0, step - 1, t], target)
            send(xt_send.at[t, to_x], xt_recv.at[t, step - 1], s_t.at[1, step - 1, t], r_t.at[1, step - 1, t], target)

    last = []

    def finish(t):
        mixed = part_sum[t, me]
        total = part_total[t, me]
        for step in (1, 3, 2):
            landed(x_recv.at[t, step - 1], r_t.at[0, step - 1, t])
            landed(xt_recv.at[t, step - 1], r_t.at[1, step - 1, t])
            mixed = mixed + x_recv[t, step - 1].astype(jnp.float32)
            total = total + xt_recv[t, step - 1]
        from_z = source_z(t)
        start = (y // 2 * 8 + from_z) * 256 + 64 * x
        count = sizes_ref[work_group]
        slot_lane = lax.broadcasted_iota(jnp.int32, (8, 128), 1) % 64 + start
        divisor = jnp.where(slot_lane < count, total, 1.0)
        done_log[t] = jnp.where(slot_lane < count, SCALE + jnp.log(divisor), 0.0)
        slot_row = lax.broadcasted_iota(jnp.int32, (64, 1), 0) + start
        mean = jnp.where(slot_row < count, mixed / lanes_to_rows(divisor), 0.0)
        done_rows[t] = mean.astype(jnp.bfloat16)
        target = device(work_x, y, from_z, work_core)
        mine = jnp.logical_and(is_self, from_z == z)
        pairs = ((done_rows.at[t], mean_ref.at[0, pl.ds(pl.multiple_of(64 * x, 64), 64)], 0), (done_log.at[t], home_log.at[x], 1))
        for src, dst, kind in pairs:
            remote = pltpu.make_async_remote_copy(
                src_ref=src, dst_ref=dst, send_sem=s_h.at[kind, t], recv_sem=r_h.at[kind, x],
                device_id=target, device_id_type=MESH,
            )
            local = pltpu.make_async_copy(src, dst, r_h.at[kind, x])
            last.append((mine, remote))

            @pl.when(mine)
            def _():
                local.start()

            @pl.when(jnp.logical_not(mine))
            def _():
                remote.start()

    for t in range(6):
        if t < 4:
            compute(t)
        if 1 <= t < 5:
            to_owner(t - 1)
        if t >= 2:
            finish(t - 2)

    for quarter in range(4):
        landed(mean_ref.at[0, pl.ds(64 * quarter, 64)], r_h.at[0, quarter])
        landed(home_log.at[quarter], r_h.at[1, quarter])
    log_ref[...] = jnp.concatenate(
        [jnp.where(low, home_log[0], home_log[1])[0:1], jnp.where(low, home_log[2], home_log[3])[0:1]], axis=1
    )
    for copy in sent:
        copy.wait_send()
    for mine, remote in first + last:

        @pl.when(jnp.logical_not(mine))
        def _():
            remote.wait_send()


def per_device(member_embed, sizes, order, ref_embed):
    vmem = pl.BlockSpec(memory_space=pltpu.VMEM)
    anywhere = pl.BlockSpec(memory_space=pl.ANY)
    bf16, f32 = jnp.bfloat16, jnp.float32
    dma = pltpu.SemaphoreType.DMA
    return pl.pallas_call(
        kernel,
        out_shape=(jax.ShapeDtypeStruct((1, 256), f32), jax.ShapeDtypeStruct((1, 256, 768), bf16)),
        in_specs=[anywhere, pl.BlockSpec(memory_space=pltpu.SMEM), vmem, anywhere],
        out_specs=(vmem, vmem),
        scratch_shapes=[
            pltpu.VMEM((256, 768), f32),
            pltpu.VMEM((16, 32, 768), f32),
            pltpu.VMEM((256, 768), bf16),
            pltpu.VMEM((4, 8, 128), f32),
            pltpu.VMEM((16, 32, 768), bf16),
            pltpu.VMEM((4, 8, 64, 768), bf16),
            pltpu.VMEM((4, 8, 8, 128), f32),
            pltpu.VMEM((2, 4, 64, 768), bf16),
            pltpu.VMEM((4, 8, 128), f32),
            pltpu.VMEM((8, 32, 768), bf16),
            pltpu.VMEM((8, 4, 32, 768), bf16),
            pltpu.VMEM((4, 8, 64, 768), f32),
            pltpu.VMEM((4, 8, 8, 128), f32),
            pltpu.VMEM((4, 4, 64, 768), bf16),
            pltpu.VMEM((4, 4, 64, 768), bf16),
            pltpu.VMEM((4, 4, 8, 128), f32),
            pltpu.VMEM((4, 4, 8, 128), f32),
            pltpu.VMEM((8, 128), f32),
            pltpu.VMEM((8, 128), f32),
            pltpu.VMEM((4, 4, 64, 768), bf16),
            pltpu.VMEM((4, 3, 64, 768), bf16),
            pltpu.VMEM((4, 4, 8, 128), f32),
            pltpu.VMEM((4, 3, 8, 128), f32),
            pltpu.VMEM((4, 64, 768), bf16),
            pltpu.VMEM((4, 8, 128), f32),
            pltpu.VMEM((4, 8, 128), f32),
            dma((2,)),
            dma((2, 4)), dma((2, 4)),
            dma((2, 3, 4)), dma((2, 3, 4)),
            dma((2, 4)), dma((2, 4)),
            dma((2, 4)), dma((2, 4)),
            dma((2, 8)), dma((2, 8)),
            dma((3, 8)), dma((3, 8)),
            dma((2, 4)), dma((2, 4)),
            dma((2, 3, 4)), dma((2, 3, 4)),
            dma((2, 4)), dma((2, 4)),
        ],
        compiler_params=pltpu.CompilerParams(
            collective_id=0, has_side_effects=True, vmem_limit_bytes=56 * 1024 * 1024
        ),
        cost_estimate=pl.CostEstimate(flops=4 * 2048 * 1536 * 768, bytes_accessed=4 << 20, transcendentals=2048 * 1536),
        name="dedup_scores",
    )(member_embed, sizes, order, ref_embed)


def solution(mesh):
    placed = (P("grp", "blk", None), P(), P("grp", "blk"), P(None, ("grp", "blk"), None))
    return jax.shard_map(
        per_device,
        mesh=mesh,
        in_specs=placed,
        out_specs=(P("grp", "blk"), P("grp", "blk", None)),
        check_vma=False,
    )
```

```python
import functools
import math

import jax
import jax.numpy as jnp
from jax import lax
from jax.experimental import pallas as pl
from jax.experimental.pallas import tpu as pltpu
from jax.sharding import PartitionSpec as P

SCALE = 32
MESH = pl.DeviceIdType.MESH
LOG2E = math.log2(math.e)
STEPS = (0, 4, 1, 7, 2, 6, 3, 5)


def unit_rows(values):
    mean_square = jnp.mean(values * values, axis=-1, keepdims=True)
    return (values * lax.rsqrt(mean_square + 1e-06)).astype(jnp.bfloat16)


def device(x, y, z, core):
    return ((x * 2 + y % 2) * 2 + core, (y // 2) * 8 + z)


def lanes_to_rows(tile):
    wide = jnp.concatenate([tile] * 8, axis=0)
    row = lax.broadcasted_iota(jnp.int32, (64, 128), 0)
    lane = lax.broadcasted_iota(jnp.int32, (64, 128), 1)
    return jnp.sum(jnp.where(row == lane, wide, 0.0), axis=1, keepdims=True)


def rows_to_lanes(column):
    row = lax.broadcasted_iota(jnp.int32, (64, 128), 0)
    lane = lax.broadcasted_iota(jnp.int32, (64, 128), 1)
    spread = jnp.where(row == lane % 64, jnp.broadcast_to(column, (64, 128)), 0.0)
    return jnp.broadcast_to(jnp.sum(spread, axis=0, keepdims=True), (8, 128))


def slot_position(delta):
    return delta + delta // 2 - 2 * (delta // 3)


def kernel(
    member_hbm, sizes_ref, order_ref, ref_hbm, log_ref, mean_ref,
    member_in, ref_in, home_rows, home_rank, hop_rows, hop_rank, ref_unit, query, rank, key_member, rank_partner, ref_other, key_ref,
    part_sum, part_total, lane_total, mix_send, mix_recv, tot_send, tot_recv, own_mix, own_tot,
    x_send, x_recv, xt_send, xt_recv, done_rows, done_log, home_log,
    load_sem, s_q, r_q, s_a, r_a, s_x, r_x, s_c, r_c, s_y, r_y, s_z, r_z, s_ry, r_ry,
    s_m, r_m, s_t, r_t, s_h, r_h,
):
    g = lax.axis_index("grp")
    b = lax.axis_index("blk")
    x, y, z, core = g // 4, (b // 8) * 2 + (g // 2) % 2, b % 8, g % 2
    parity = y % 2
    other = 1 - core
    home_z = 2 * x + core
    work_x, work_core = z // 2, z % 2
    is_self = home_z == z
    stays = z % 2 == core
    work_group = (work_x * 2 + parity) * 2 + work_core

    z_steps = [(step + core * (8 - 2 * step)) % 8 for step in STEPS]
    x_steps = [step + core * (4 - 2 * step) for step in (2, 1, 3)]

    def source_z(position):
        return 2 * ((z // 2 + slot_position(position)) % 4) + core

    load_members = pltpu.make_async_copy(member_hbm.at[0], member_in, load_sem.at[0])
    load_refs = pltpu.make_async_copy(ref_hbm, ref_in, load_sem.at[1])
    load_members.start()
    load_refs.start()

    barrier = pltpu.get_barrier_semaphore()

    def greet(target):
        pl.semaphore_signal(barrier, inc=1, device_id=target, device_id_type=MESH)

    for step in (1, 2, 3):
        greet(device((x + step) % 4, y, z, core))
        greet(device(x, (y + step) % 4, z, core))
    for step in range(1, 8):
        greet(device(x, y, (z + step) % 8, core))
    greet(device(x, y, z, other))
    for position in range(4):
        from_z = source_z(position)

        @pl.when(jnp.logical_not(jnp.logical_and(stays, from_z == z)))
        def _():
            greet(device(x, y, from_z, z % 2))

    for quarter in range(4):

        @pl.when(jnp.logical_not(jnp.logical_and(is_self, x == quarter)))
        def _():
            greet(device(quarter, y, home_z, z % 2))

    load_members.wait()
    home_rows[...] = unit_rows(member_in[...])
    live_count = sizes_ref[g]
    slot = lax.broadcasted_iota(jnp.int32, (1, 256), 1) + b * 256
    ranks = jnp.where(slot < live_count, order_ref[...], 4096).astype(jnp.float32)
    for quarter in range(4):
        piece = ranks[:, 64 * quarter : 64 * quarter + 64]
        home_rank[quarter] = jnp.broadcast_to(jnp.concatenate([piece, piece], axis=1), (8, 128))

    load_refs.wait()
    for group in range(4):
        ref_unit[pl.ds(4 * group, 4)] = unit_rows(ref_in[pl.ds(4 * group, 4)])

    pl.semaphore_wait(barrier, 22 - is_self.astype(jnp.int32) - stays.astype(jnp.int32))

    sent = []

    def send(src, dst, send_sem, recv_sem, target):
        copy = pltpu.make_async_remote_copy(
            src_ref=src, dst_ref=dst, send_sem=send_sem, recv_sem=recv_sem, device_id=target, device_id_type=MESH
        )
        copy.start()
        sent.append(copy)
        return copy

    def landed(dst, sem):
        pltpu.make_async_copy(dst, dst, sem).wait()

    for i, step in enumerate(x_steps):
        to_x = (x + step) % 4
        target = device(to_x, y, z, core)
        quarter = pl.ds(pl.multiple_of(64 * to_x, 64), 64)
        send(home_rows.at[quarter], hop_rows.at[i], s_q.at[0, i], r_q.at[0, i], target)
        send(home_rank.at[to_x], hop_rank.at[i], s_q.at[1, i], r_q.at[1, i], target)

    row_owner = z % 2 * 4 + x
    first = []

    def to_row(i):
        from_x = (x + 4 - x_steps[i]) % 4 if i < 3 else x
        to_z = 2 * from_x + core
        here = slot_position((z // 2 - from_x + 4) % 4)
        if i < 3:
            rows, ranks = hop_rows.at[i], hop_rank.at[i]
            landed(rows, r_q.at[0, i])
            landed(ranks, r_q.at[1, i])
        else:
            rows, ranks = home_rows.at[pl.ds(pl.multiple_of(64 * x, 64), 64)], home_rank.at[x]
        mine = to_z == z
        for src, dst, kind in ((rows, query.at[here, row_owner], 0), (ranks, rank.at[here, row_owner], 1)):
            remote = pltpu.make_async_remote_copy(
                src_ref=src, dst_ref=dst, send_sem=s_a.at[kind, i], recv_sem=r_a.at[kind, here],
                device_id=device(x, y, to_z, z % 2), device_id_type=MESH,
            )
            local = pltpu.make_async_copy(src, dst, r_a.at[kind, here])
            first.append((mine, remote))

            @pl.when(mine)
            def _():
                local.start()

            @pl.when(jnp.logical_not(mine))
            def _():
                remote.start()

    def ref_index(to_z, side):
        return (to_z // 2) * 4 + side * 2 + to_z % 2

    key_ref[0, 0] = ref_unit[ref_index(z, parity)]
    ref_other[0] = ref_unit[ref_index(z, 1 - parity)]
    def send_refs(i):
        to_z = (z + 8 - z_steps[i]) % 8
        target = device(x, y, to_z, core)
        send(ref_unit.at[ref_index(to_z, parity)], key_ref.at[i, 0], s_z.at[0, i], r_z.at[0, i], target)
        send(ref_unit.at[ref_index(to_z, 1 - parity)], ref_other.at[i], s_z.at[1, i], r_z.at[1, i], target)

    opposite = device(x, (y + 2) % 4, z, core)
    above = device(x, (y + 1) % 4, z, core)
    below = device(x, (y + 3) % 4, z, core)

    def pass_refs(i):
        if i:
            landed(key_ref.at[i, 0], r_z.at[0, i])
            landed(ref_other.at[i], r_z.at[1, i])
        send(key_ref.at[i, 0], key_ref.at[i, 1], s_ry.at[0, i], r_ry.at[0, i], opposite)
        send(ref_other.at[i], key_ref.at[i, 2], s_ry.at[1, i], r_ry.at[1, i], above)
        send(ref_other.at[i], key_ref.at[i, 3], s_ry.at[2, i], r_ry.at[2, i], below)

    me = core * 4 + x

    def pass_queries(t):
        landed(query.at[t, me], r_a.at[0, t])
        landed(rank.at[t, me], r_a.at[1, t])
        for i, step in enumerate(x_steps):
            target = device((x + step) % 4, y, z, core)
            send(query.at[t, me], query.at[t, me], s_x.at[0, i, t], r_x.at[0, i, t], target)
            send(rank.at[t, me], rank.at[t, me], s_x.at[1, i, t], r_x.at[1, i, t], target)
        send(query.at[t, me], key_member.at[1, t], s_y.at[0, t], r_y.at[0, t], opposite)
        send(rank.at[t, me], rank_partner.at[t], s_y.at[1, t], r_y.at[1, t], opposite)
        key_member[0, t] = query[t, me]

    sibling = device(x, y, z, other)
    my_half, other_half = pl.ds(core * 4, 4), pl.ds(other * 4, 4)

    def share_queries(t):
        for i in (1, 2, 0):
            from_x = core * 4 + (x + 4 - x_steps[i]) % 4
            landed(query.at[t, from_x], r_x.at[0, i, t])
            landed(rank.at[t, from_x], r_x.at[1, i, t])
        send(query.at[t, my_half], query.at[t, my_half], s_c.at[0, t], r_c.at[0, t], sibling)
        send(rank.at[t, my_half], rank.at[t, my_half], s_c.at[1, t], r_c.at[1, t], sibling)

    low = lax.broadcasted_iota(jnp.int32, (8, 128), 1) < 64

    def queries_landed(t):
        landed(query.at[t, other_half], r_c.at[0, t])
        landed(rank.at[t, other_half], r_c.at[1, t])

    def members_landed():
        for t in range(4):
            landed(key_member.at[1, t], r_y.at[0, t])
            landed(rank_partner.at[t], r_y.at[1, t])

    def refs_landed(half):
        for i in range(4 * half, 4 * half + 4):
            for side in range(3):
                landed(key_ref.at[i, side + 1], r_ry.at[side, i])

    def weigh(t, keys):
        logits = lax.dot_general(
            query[t].reshape(512, 768), keys, (((1,), (1,)), ((), ())), preferred_element_type=jnp.float32
        )
        return jnp.exp2(logits * (SCALE / 768 * LOG2E) - SCALE * LOG2E)

    def lane_sums(weight):
        return weight[:, 0:128] + weight[:, 128:256] + weight[:, 256:384] + weight[:, 384:512]

    begun = set()

    def add_up(t, weight, keys):
        mixed = jnp.dot(weight.astype(jnp.bfloat16), keys, preferred_element_type=jnp.float32).reshape(8, 64, 768)
        if t in begun:
            lane_total[t] += lane_sums(weight)
            part_sum[t] += mixed
        else:
            lane_total[t] = lane_sums(weight)
            part_sum[t] = mixed
            begun.add(t)

    def compute_members(t):
        key_rank = jnp.concatenate(
            [
                jnp.where(low, rank[0, me], rank[1, me]),
                jnp.where(low, rank[2, me], rank[3, me]),
                jnp.where(low, rank_partner[0], rank_partner[1]),
                jnp.where(low, rank_partner[2], rank_partner[3]),
            ],
            axis=1,
        )[0:1]
        row_rank = jnp.concatenate([lanes_to_rows(rank[t, owner]) for owner in range(8)], axis=0)
        keys = key_member[...].reshape(512, 768)
        weight = jnp.where(key_rank < row_rank, weigh(t, keys), 0.0)
        add_up(t, weight, keys)

    def compute_refs(t, half):
        keys = key_ref[pl.ds(4 * half, 4)].reshape(512, 768)
        weight = weigh(t, keys)
        add_up(t, weight, keys)

    def to_sibling(t):
        total = jnp.sum(lane_total[t], axis=1, keepdims=True)
        for owner in range(8):
            part_total[t, owner] = rows_to_lanes(total[64 * owner : 64 * owner + 64])
        mix_send[t] = part_sum[t, other_half].astype(jnp.bfloat16)
        tot_send[t] = part_total[t, other_half]
        send(mix_send.at[t], mix_recv.at[t], s_m.at[0, t], r_m.at[0, t], sibling)
        send(tot_send.at[t], tot_recv.at[t], s_m.at[1, t], r_m.at[1, t], sibling)

    def to_owner(t):
        landed(mix_recv.at[t], r_m.at[0, t])
        landed(tot_recv.at[t], r_m.at[1, t])
        mixed = part_sum[t, my_half] + mix_recv[t].astype(jnp.float32)
        total = part_total[t, my_half] + tot_recv[t]
        part_sum[t, my_half] = mixed
        part_total[t, my_half] = total
        x_send[t] = mixed.astype(jnp.bfloat16)
        xt_send[t] = total
        for i, step in enumerate(x_steps):
            to_x = (x + step) % 4
            target = device(to_x, y, z, core)
            send(x_send.at[t, to_x], x_recv.at[t, i], s_t.at[0, i, t], r_t.at[0, i, t], target)
            send(xt_send.at[t, to_x], xt_recv.at[t, i], s_t.at[1, i, t], r_t.at[1, i, t], target)

    last = []

    def finish(t):
        mixed = part_sum[t, me]
        total = part_total[t, me]
        for i in (1, 2, 0):
            landed(x_recv.at[t, i], r_t.at[0, i, t])
            landed(xt_recv.at[t, i], r_t.at[1, i, t])
            mixed = mixed + x_recv[t, i].astype(jnp.float32)
            total = total + xt_recv[t, i]
        from_z = source_z(t)
        start = (y // 2 * 8 + from_z) * 256 + 64 * x
        count = sizes_ref[work_group]
        slot_lane = lax.broadcasted_iota(jnp.int32, (8, 128), 1) % 64 + start
        divisor = jnp.where(slot_lane < count, total, 1.0)
        done_log[t] = jnp.where(slot_lane < count, SCALE + jnp.log(divisor), 0.0)
        slot_row = lax.broadcasted_iota(jnp.int32, (64, 1), 0) + start
        mean = jnp.where(slot_row < count, mixed / lanes_to_rows(divisor), 0.0)
        done_rows[t] = mean.astype(jnp.bfloat16)
        target = device(work_x, y, from_z, work_core)
        mine = jnp.logical_and(is_self, from_z == z)
        pairs = ((done_rows.at[t], mean_ref.at[0, pl.ds(pl.multiple_of(64 * x, 64), 64)], 0), (done_log.at[t], home_log.at[x], 1))
        for src, dst, kind in pairs:
            remote = pltpu.make_async_remote_copy(
                src_ref=src, dst_ref=dst, send_sem=s_h.at[kind, t], recv_sem=r_h.at[kind, x],
                device_id=target, device_id_type=MESH,
            )
            local = pltpu.make_async_copy(src, dst, r_h.at[kind, x])
            last.append((mine, remote))

            @pl.when(mine)
            def _():
                local.start()

            @pl.when(jnp.logical_not(mine))
            def _():
                remote.start()

    send_refs(1)
    pass_refs(0)
    to_row(3)
    to_row(1)
    to_row(2)
    to_row(0)
    send_refs(2)
    send_refs(3)
    send_refs(4)
    send_refs(5)
    send_refs(6)
    send_refs(7)
    pass_queries(0)
    pass_refs(1)
    pass_queries(1)
    pass_queries(2)
    pass_refs(2)
    pass_refs(3)
    share_queries(0)
    pass_queries(3)
    pass_refs(4)
    pass_refs(5)
    share_queries(1)
    share_queries(2)
    queries_landed(0)
    refs_landed(0)
    compute_refs(0, 0)
    queries_landed(1)
    compute_refs(1, 0)
    pass_refs(6)
    queries_landed(2)
    compute_refs(2, 0)
    pass_refs(7)
    share_queries(3)
    members_landed()
    compute_members(0)
    compute_members(1)
    compute_members(2)
    queries_landed(3)
    compute_refs(3, 0)
    compute_members(3)
    refs_landed(1)
    compute_refs(0, 1)
    to_sibling(0)
    compute_refs(1, 1)
    to_sibling(1)
    to_owner(0)
    compute_refs(2, 1)
    to_sibling(2)
    to_owner(1)
    compute_refs(3, 1)
    to_sibling(3)
    to_owner(2)
    to_owner(3)
    finish(0)
    finish(1)
    finish(2)
    finish(3)

    for quarter in range(4):
        landed(mean_ref.at[0, pl.ds(64 * quarter, 64)], r_h.at[0, quarter])
        landed(home_log.at[quarter], r_h.at[1, quarter])
    log_ref[...] = jnp.concatenate(
        [jnp.where(low, home_log[0], home_log[1])[0:1], jnp.where(low, home_log[2], home_log[3])[0:1]], axis=1
    )
    for copy in sent:
        copy.wait_send()
    for mine, remote in first + last:

        @pl.when(jnp.logical_not(mine))
        def _():
            remote.wait_send()


def per_device(member_embed, sizes, order, ref_embed):
    vmem = pl.BlockSpec(memory_space=pltpu.VMEM)
    anywhere = pl.BlockSpec(memory_space=pl.ANY)
    bf16, f32 = jnp.bfloat16, jnp.float32
    dma = pltpu.SemaphoreType.DMA
    return pl.pallas_call(
        kernel,
        out_shape=(jax.ShapeDtypeStruct((1, 256), f32), jax.ShapeDtypeStruct((1, 256, 768), bf16)),
        in_specs=[anywhere, pl.BlockSpec(memory_space=pltpu.SMEM), vmem, anywhere],
        out_specs=(vmem, vmem),
        scratch_shapes=[
            pltpu.VMEM((256, 768), f32),
            pltpu.VMEM((16, 32, 768), f32),
            pltpu.VMEM((256, 768), bf16),
            pltpu.VMEM((4, 8, 128), f32),
            pltpu.VMEM((3, 64, 768), bf16),
            pltpu.VMEM((3, 8, 128), f32),
            pltpu.VMEM((16, 32, 768), bf16),
            pltpu.VMEM((4, 8, 64, 768), bf16),
            pltpu.VMEM((4, 8, 8, 128), f32),
            pltpu.VMEM((2, 4, 64, 768), bf16),
            pltpu.VMEM((4, 8, 128), f32),
            pltpu.VMEM((8, 32, 768), bf16),
            pltpu.VMEM((8, 4, 32, 768), bf16),
            pltpu.VMEM((4, 8, 64, 768), f32),
            pltpu.VMEM((4, 8, 8, 128), f32),
            pltpu.VMEM((4, 512, 128), f32),
            pltpu.VMEM((4, 4, 64, 768), bf16),
            pltpu.VMEM((4, 4, 64, 768), bf16),
            pltpu.VMEM((4, 4, 8, 128), f32),
            pltpu.VMEM((4, 4, 8, 128), f32),
            pltpu.VMEM((8, 128), f32),
            pltpu.VMEM((8, 128), f32),
            pltpu.VMEM((4, 4, 64, 768), bf16),
            pltpu.VMEM((4, 3, 64, 768), bf16),
            pltpu.VMEM((4, 4, 8, 128), f32),
            pltpu.VMEM((4, 3, 8, 128), f32),
            pltpu.VMEM((4, 64, 768), bf16),
            pltpu.VMEM((4, 8, 128), f32),
            pltpu.VMEM((4, 8, 128), f32),
            dma((2,)),
            dma((2, 3)), dma((2, 3)),
            dma((2, 4)), dma((2, 4)),
            dma((2, 3, 4)), dma((2, 3, 4)),
            dma((2, 4)), dma((2, 4)),
            dma((2, 4)), dma((2, 4)),
            dma((2, 8)), dma((2, 8)),
            dma((3, 8)), dma((3, 8)),
            dma((2, 4)), dma((2, 4)),
            dma((2, 3, 4)), dma((2, 3, 4)),
            dma((2, 4)), dma((2, 4)),
        ],
        compiler_params=pltpu.CompilerParams(
            collective_id=0, has_side_effects=True, vmem_limit_bytes=56 * 1024 * 1024
        ),
        cost_estimate=pl.CostEstimate(flops=4 * 2048 * 1536 * 768, bytes_accessed=4 << 20, transcendentals=2048 * 1536),
        name="dedup_scores",
    )(member_embed, sizes, order, ref_embed)


def solution(mesh):
    placed = (P("grp", "blk", None), P(), P("grp", "blk"), P(None, ("grp", "blk"), None))
    return jax.shard_map(
        per_device,
        mesh=mesh,
        in_specs=placed,
        out_specs=(P("grp", "blk"), P("grp", "blk", None)),
        check_vma=False,
    )
```

```python
import functools
import math

import jax
import jax.numpy as jnp
from jax import lax
from jax.experimental import pallas as pl
from jax.experimental.pallas import tpu as pltpu
from jax.sharding import PartitionSpec as P

SCALE = 32
MESH = pl.DeviceIdType.MESH
LOG2E = math.log2(math.e)
STEPS = (0, 2, 6, 1, 7, 3, 5, 4)


def unit_rows(values):
    mean_square = jnp.mean(values * values, axis=-1, keepdims=True)
    return (values * lax.rsqrt(mean_square + 1e-06)).astype(jnp.bfloat16)


def device(x, y, z, core):
    return ((x * 2 + y % 2) * 2 + core, (y // 2) * 8 + z)


def lanes_to_rows(tile):
    wide = jnp.concatenate([tile] * 8, axis=0)
    row = lax.broadcasted_iota(jnp.int32, (64, 128), 0)
    lane = lax.broadcasted_iota(jnp.int32, (64, 128), 1)
    return jnp.sum(jnp.where(row == lane, wide, 0.0), axis=1, keepdims=True)


def rows_to_lanes(column):
    row = lax.broadcasted_iota(jnp.int32, (64, 128), 0)
    lane = lax.broadcasted_iota(jnp.int32, (64, 128), 1)
    spread = jnp.where(row == lane % 64, jnp.broadcast_to(column, (64, 128)), 0.0)
    return jnp.broadcast_to(jnp.sum(spread, axis=0, keepdims=True), (8, 128))


def slot_position(delta):
    return delta + delta // 2 - 2 * (delta // 3)


def kernel(
    member_hbm, sizes_ref, order_ref, ref_hbm, log_ref, mean_ref,
    member_in, ref_in, home_rows, home_rank, hop_rows, hop_rank, ref_unit, query, rank, key_member, rank_partner, ref_other, key_ref,
    part_sum, part_total, lane_total, mix_send, mix_recv, tot_send, tot_recv, own_mix, own_tot,
    x_send, x_recv, xt_send, xt_recv, chain_rows, chain_total, done_rows, done_log, home_log,
    load_sem, s_q, r_q, s_a, r_a, s_x, r_x, s_c, r_c, s_y, r_y, s_z, r_z, s_ry, r_ry,
    s_m, r_m, s_t, r_t, s_h, r_h,
):
    g = lax.axis_index("grp")
    b = lax.axis_index("blk")
    x, y, z, core = g // 4, (b // 8) * 2 + (g // 2) % 2, b % 8, g % 2
    parity = y % 2
    other = 1 - core
    home_z = 2 * x + core
    work_x, work_core = z // 2, z % 2
    is_self = home_z == z
    stays = z % 2 == core
    work_group = (work_x * 2 + parity) * 2 + work_core

    z_steps = [(step + core * (8 - 2 * step)) % 8 for step in STEPS]
    x_steps = [step + core * (4 - 2 * step) for step in (2, 1, 3)]

    def source_z(position):
        return 2 * ((z // 2 + slot_position(position)) % 4) + core

    load_members = pltpu.make_async_copy(member_hbm.at[0], member_in, load_sem.at[0])
    load_refs = pltpu.make_async_copy(ref_hbm, ref_in, load_sem.at[1])
    load_members.start()
    load_refs.start()

    barrier = pltpu.get_barrier_semaphore()

    def greet(target):
        pl.semaphore_signal(barrier, inc=1, device_id=target, device_id_type=MESH)

    for step in (1, 2, 3):
        greet(device((x + step) % 4, y, z, core))
        greet(device(x, (y + step) % 4, z, core))
    for step in range(1, 8):
        greet(device(x, y, (z + step) % 8, core))
    greet(device(x, y, z, other))
    for position in range(4):
        from_z = source_z(position)

        @pl.when(jnp.logical_not(jnp.logical_and(stays, from_z == z)))
        def _():
            greet(device(x, y, from_z, z % 2))

    for quarter in range(4):

        @pl.when(jnp.logical_not(jnp.logical_and(is_self, x == quarter)))
        def _():
            greet(device(quarter, y, home_z, z % 2))

    load_members.wait()
    home_rows[...] = unit_rows(member_in[...])
    live_count = sizes_ref[g]
    slot = lax.broadcasted_iota(jnp.int32, (1, 256), 1) + b * 256
    ranks = jnp.where(slot < live_count, order_ref[...], 4096).astype(jnp.float32)
    for quarter in range(4):
        piece = ranks[:, 64 * quarter : 64 * quarter + 64]
        home_rank[quarter] = jnp.broadcast_to(jnp.concatenate([piece, piece], axis=1), (8, 128))

    load_refs.wait()
    for group in range(4):
        ref_unit[pl.ds(4 * group, 4)] = unit_rows(ref_in[pl.ds(4 * group, 4)])

    pl.semaphore_wait(barrier, 22 - is_self.astype(jnp.int32) - stays.astype(jnp.int32))

    sent = []

    def send(src, dst, send_sem, recv_sem, target):
        copy = pltpu.make_async_remote_copy(
            src_ref=src, dst_ref=dst, send_sem=send_sem, recv_sem=recv_sem, device_id=target, device_id_type=MESH
        )
        copy.start()
        sent.append(copy)
        return copy

    def landed(dst, sem):
        pltpu.make_async_copy(dst, dst, sem).wait()

    for i, step in enumerate(x_steps):
        to_x = (x + step) % 4
        target = device(to_x, y, z, core)
        quarter = pl.ds(pl.multiple_of(64 * to_x, 64), 64)
        send(home_rows.at[quarter], hop_rows.at[i], s_q.at[0, i], r_q.at[0, i], target)
        send(home_rank.at[to_x], hop_rank.at[i], s_q.at[1, i], r_q.at[1, i], target)

    row_owner = z % 2 * 4 + x
    first = []

    def to_row(i):
        from_x = (x + 4 - x_steps[i]) % 4 if i < 3 else x
        to_z = 2 * from_x + core
        here = slot_position((z // 2 - from_x + 4) % 4)
        if i < 3:
            rows, ranks = hop_rows.at[i], hop_rank.at[i]
            landed(rows, r_q.at[0, i])
            landed(ranks, r_q.at[1, i])
        else:
            rows, ranks = home_rows.at[pl.ds(pl.multiple_of(64 * x, 64), 64)], home_rank.at[x]
        mine = to_z == z
        for src, dst, kind in ((rows, query.at[here, row_owner], 0), (ranks, rank.at[here, row_owner], 1)):
            remote = pltpu.make_async_remote_copy(
                src_ref=src, dst_ref=dst, send_sem=s_a.at[kind, i], recv_sem=r_a.at[kind, here],
                device_id=device(x, y, to_z, z % 2), device_id_type=MESH,
            )
            local = pltpu.make_async_copy(src, dst, r_a.at[kind, here])
            first.append((mine, remote))

            @pl.when(mine)
            def _():
                local.start()

            @pl.when(jnp.logical_not(mine))
            def _():
                remote.start()

    def ref_index(to_z, side):
        return (to_z // 2) * 4 + side * 2 + to_z % 2

    key_ref[0, 0] = ref_unit[ref_index(z, parity)]
    ref_other[0] = ref_unit[ref_index(z, 1 - parity)]
    def send_refs(i):
        to_z = (z + 8 - z_steps[i]) % 8
        target = device(x, y, to_z, core)
        send(ref_unit.at[ref_index(to_z, parity)], key_ref.at[i, 0], s_z.at[0, i], r_z.at[0, i], target)
        send(ref_unit.at[ref_index(to_z, 1 - parity)], ref_other.at[i], s_z.at[1, i], r_z.at[1, i], target)

    opposite = device(x, (y + 2) % 4, z, core)
    above = device(x, (y + 1) % 4, z, core)
    below = device(x, (y + 3) % 4, z, core)

    def pass_refs(i):
        if i:
            landed(key_ref.at[i, 0], r_z.at[0, i])
            landed(ref_other.at[i], r_z.at[1, i])
        send(key_ref.at[i, 0], key_ref.at[i, 1], s_ry.at[0, i], r_ry.at[0, i], opposite)
        send(ref_other.at[i], key_ref.at[i, 2], s_ry.at[1, i], r_ry.at[1, i], above)
        send(ref_other.at[i], key_ref.at[i, 3], s_ry.at[2, i], r_ry.at[2, i], below)

    me = core * 4 + x

    def pass_queries(t):
        landed(query.at[t, me], r_a.at[0, t])
        landed(rank.at[t, me], r_a.at[1, t])
        for i, step in enumerate(x_steps):
            target = device((x + step) % 4, y, z, core)
            send(query.at[t, me], query.at[t, me], s_x.at[0, i, t], r_x.at[0, i, t], target)
            send(rank.at[t, me], rank.at[t, me], s_x.at[1, i, t], r_x.at[1, i, t], target)
        send(query.at[t, me], key_member.at[1, t], s_y.at[0, t], r_y.at[0, t], opposite)
        send(rank.at[t, me], rank_partner.at[t], s_y.at[1, t], r_y.at[1, t], opposite)
        key_member[0, t] = query[t, me]

    sibling = device(x, y, z, other)
    my_half, other_half = pl.ds(core * 4, 4), pl.ds(other * 4, 4)

    def share_queries(t):
        for i in (1, 2, 0):
            from_x = core * 4 + (x + 4 - x_steps[i]) % 4
            landed(query.at[t, from_x], r_x.at[0, i, t])
            landed(rank.at[t, from_x], r_x.at[1, i, t])
        send(query.at[t, my_half], query.at[t, my_half], s_c.at[0, t], r_c.at[0, t], sibling)
        send(rank.at[t, my_half], rank.at[t, my_half], s_c.at[1, t], r_c.at[1, t], sibling)

    low = lax.broadcasted_iota(jnp.int32, (8, 128), 1) < 64

    def queries_landed(t):
        landed(query.at[t, other_half], r_c.at[0, t])
        landed(rank.at[t, other_half], r_c.at[1, t])

    def members_landed():
        for t in range(4):
            landed(key_member.at[1, t], r_y.at[0, t])
            landed(rank_partner.at[t], r_y.at[1, t])

    def refs_landed(half):
        for i in range(4 * half, 4 * half + 4):
            for side in range(3):
                landed(key_ref.at[i, side + 1], r_ry.at[side, i])

    def weigh(t, keys):
        logits = lax.dot_general(
            query[t].reshape(512, 768), keys, (((1,), (1,)), ((), ())), preferred_element_type=jnp.float32
        )
        return jnp.exp2(logits * (SCALE / 768 * LOG2E) - SCALE * LOG2E)

    def lane_sums(weight):
        return weight[:, 0:128] + weight[:, 128:256] + weight[:, 256:384] + weight[:, 384:512]

    begun = set()

    def add_up(t, weight, keys):
        mixed = jnp.dot(weight.astype(jnp.bfloat16), keys, preferred_element_type=jnp.float32).reshape(8, 64, 768)
        if t in begun:
            lane_total[t] += lane_sums(weight)
            part_sum[t] += mixed
        else:
            lane_total[t] = lane_sums(weight)
            part_sum[t] = mixed
            begun.add(t)

    def compute_members(t):
        key_rank = jnp.concatenate(
            [
                jnp.where(low, rank[0, me], rank[1, me]),
                jnp.where(low, rank[2, me], rank[3, me]),
                jnp.where(low, rank_partner[0], rank_partner[1]),
                jnp.where(low, rank_partner[2], rank_partner[3]),
            ],
            axis=1,
        )[0:1]
        row_rank = jnp.concatenate([lanes_to_rows(rank[t, owner]) for owner in range(8)], axis=0)
        keys = key_member[...].reshape(512, 768)
        weight = jnp.where(key_rank < row_rank, weigh(t, keys), 0.0)
        add_up(t, weight, keys)

    def compute_refs(t, half):
        keys = key_ref[pl.ds(4 * half, 4)].reshape(512, 768)
        weight = weigh(t, keys)
        add_up(t, weight, keys)

    def to_sibling(t):
        total = jnp.sum(lane_total[t], axis=1, keepdims=True)
        for owner in range(8):
            part_total[t, owner] = rows_to_lanes(total[64 * owner : 64 * owner + 64])
        mix_send[t] = part_sum[t, other_half].astype(jnp.bfloat16)
        tot_send[t] = part_total[t, other_half]
        send(mix_send.at[t], mix_recv.at[t], s_m.at[0, t], r_m.at[0, t], sibling)
        send(tot_send.at[t], tot_recv.at[t], s_m.at[1, t], r_m.at[1, t], sibling)

    def to_owner(t):
        landed(mix_recv.at[t], r_m.at[0, t])
        landed(tot_recv.at[t], r_m.at[1, t])
        mixed = part_sum[t, my_half] + mix_recv[t].astype(jnp.float32)
        total = part_total[t, my_half] + tot_recv[t]
        part_sum[t, my_half] = mixed
        part_total[t, my_half] = total
        x_send[t] = mixed.astype(jnp.bfloat16)
        xt_send[t] = total
        if t == 3:
            for i, step in enumerate(x_steps):
                send_part(t, i, x_send.at[t, (x + step) % 4], xt_send.at[t, (x + step) % 4], (x + step) % 4)
        else:
            far, near = (x + 2) % 4, (x + 4 - onward) % 4
            send_part(t, 0, x_send.at[t, far], xt_send.at[t, far], (x + onward) % 4)
            send_part(t, 1, x_send.at[t, near], xt_send.at[t, near], near)

    onward = x_steps[1]

    def send_part(t, i, rows, total, to_x):
        target = device(to_x, y, z, core)
        send(rows, x_recv.at[t, i], s_t.at[0, i, t], r_t.at[0, i, t], target)
        send(total, xt_recv.at[t, i], s_t.at[1, i, t], r_t.at[1, i, t], target)

    def part_landed(t, i):
        landed(x_recv.at[t, i], r_t.at[0, i, t])
        landed(xt_recv.at[t, i], r_t.at[1, i, t])

    def add_onward(t):
        part_landed(t, 0)
        to_x = (x + onward) % 4
        owner = core * 4 + to_x
        chain_rows[t] = (part_sum[t, owner] + x_recv[t, 0].astype(jnp.float32)).astype(jnp.bfloat16)
        chain_total[t] = part_total[t, owner] + xt_recv[t, 0]
        send_part(t, 2, chain_rows.at[t], chain_total.at[t], to_x)

    last = []

    def finish(t):
        mixed = part_sum[t, me]
        total = part_total[t, me]
        for i in (1, 2, 0) if t == 3 else (1, 2):
            part_landed(t, i)
            mixed = mixed + x_recv[t, i].astype(jnp.float32)
            total = total + xt_recv[t, i]
        from_z = source_z(t)
        start = (y // 2 * 8 + from_z) * 256 + 64 * x
        count = sizes_ref[work_group]
        slot_lane = lax.broadcasted_iota(jnp.int32, (8, 128), 1) % 64 + start
        divisor = jnp.where(slot_lane < count, total, 1.0)
        done_log[t] = jnp.where(slot_lane < count, SCALE + jnp.log(divisor), 0.0)
        slot_row = lax.broadcasted_iota(jnp.int32, (64, 1), 0) + start
        mean = jnp.where(slot_row < count, mixed / lanes_to_rows(divisor), 0.0)
        done_rows[t] = mean.astype(jnp.bfloat16)
        target = device(work_x, y, from_z, work_core)
        mine = jnp.logical_and(is_self, from_z == z)
        pairs = ((done_rows.at[t], mean_ref.at[0, pl.ds(pl.multiple_of(64 * x, 64), 64)], 0), (done_log.at[t], home_log.at[x], 1))
        for src, dst, kind in pairs:
            remote = pltpu.make_async_remote_copy(
                src_ref=src, dst_ref=dst, send_sem=s_h.at[kind, t], recv_sem=r_h.at[kind, x],
                device_id=target, device_id_type=MESH,
            )
            local = pltpu.make_async_copy(src, dst, r_h.at[kind, x])
            last.append((mine, remote))

            @pl.when(mine)
            def _():
                local.start()

            @pl.when(jnp.logical_not(mine))
            def _():
                remote.start()

    to_row(3)
    send_refs(1)
    send_refs(2)
    pass_refs(0)
    to_row(1)
    to_row(2)
    to_row(0)
    send_refs(3)
    send_refs(4)
    send_refs(5)
    send_refs(6)
    send_refs(7)
    pass_queries(0)
    pass_refs(1)
    pass_refs(2)
    pass_queries(1)
    pass_queries(2)
    pass_refs(3)
    pass_refs(4)
    share_queries(0)
    pass_queries(3)
    share_queries(1)
    share_queries(2)
    pass_refs(5)
    pass_refs(6)
    queries_landed(0)
    refs_landed(0)
    compute_refs(0, 0)
    queries_landed(1)
    compute_refs(1, 0)
    share_queries(3)
    pass_refs(7)
    queries_landed(2)
    compute_refs(2, 0)
    members_landed()
    compute_members(0)
    compute_members(1)
    compute_members(2)
    queries_landed(3)
    compute_refs(3, 0)
    compute_members(3)
    refs_landed(1)
    compute_refs(0, 1)
    to_sibling(0)
    compute_refs(1, 1)
    to_sibling(1)
    to_owner(0)
    compute_refs(2, 1)
    to_sibling(2)
    to_owner(1)
    compute_refs(3, 1)
    to_sibling(3)
    to_owner(2)
    to_owner(3)
    add_onward(0)
    add_onward(1)
    add_onward(2)
    finish(0)
    finish(1)
    finish(2)
    finish(3)

    for quarter in range(4):
        landed(mean_ref.at[0, pl.ds(64 * quarter, 64)], r_h.at[0, quarter])
        landed(home_log.at[quarter], r_h.at[1, quarter])
    log_ref[...] = jnp.concatenate(
        [jnp.where(low, home_log[0], home_log[1])[0:1], jnp.where(low, home_log[2], home_log[3])[0:1]], axis=1
    )
    for copy in sent:
        copy.wait_send()
    for mine, remote in first + last:

        @pl.when(jnp.logical_not(mine))
        def _():
            remote.wait_send()


def hand_out(log_in, mean_in, log_out, mean_out):
    log_out[...] = log_in[...]
    mean_out[...] = mean_in[...]


def per_device(member_embed, sizes, order, ref_embed):
    vmem = pl.BlockSpec(memory_space=pltpu.VMEM)
    anywhere = pl.BlockSpec(memory_space=pl.ANY)
    bf16, f32 = jnp.bfloat16, jnp.float32
    dma = pltpu.SemaphoreType.DMA
    log_total, neighbour = pl.pallas_call(
        kernel,
        out_shape=(jax.ShapeDtypeStruct((1, 256), f32), jax.ShapeDtypeStruct((1, 256, 768), bf16)),
        in_specs=[anywhere, pl.BlockSpec(memory_space=pltpu.SMEM), vmem, anywhere],
        out_specs=(vmem, vmem),
        scratch_shapes=[
            pltpu.VMEM((256, 768), f32),
            pltpu.VMEM((16, 32, 768), f32),
            pltpu.VMEM((256, 768), bf16),
            pltpu.VMEM((4, 8, 128), f32),
            pltpu.VMEM((3, 64, 768), bf16),
            pltpu.VMEM((3, 8, 128), f32),
            pltpu.VMEM((16, 32, 768), bf16),
            pltpu.VMEM((4, 8, 64, 768), bf16),
            pltpu.VMEM((4, 8, 8, 128), f32),
            pltpu.VMEM((2, 4, 64, 768), bf16),
            pltpu.VMEM((4, 8, 128), f32),
            pltpu.VMEM((8, 32, 768), bf16),
            pltpu.VMEM((8, 4, 32, 768), bf16),
            pltpu.VMEM((4, 8, 64, 768), f32),
            pltpu.VMEM((4, 8, 8, 128), f32),
            pltpu.VMEM((4, 512, 128), f32),
            pltpu.VMEM((4, 4, 64, 768), bf16),
            pltpu.VMEM((4, 4, 64, 768), bf16),
            pltpu.VMEM((4, 4, 8, 128), f32),
            pltpu.VMEM((4, 4, 8, 128), f32),
            pltpu.VMEM((8, 128), f32),
            pltpu.VMEM((8, 128), f32),
            pltpu.VMEM((4, 4, 64, 768), bf16),
            pltpu.VMEM((4, 3, 64, 768), bf16),
            pltpu.VMEM((4, 4, 8, 128), f32),
            pltpu.VMEM((4, 3, 8, 128), f32),
            pltpu.VMEM((3, 64, 768), bf16),
            pltpu.VMEM((3, 8, 128), f32),
            pltpu.VMEM((4, 64, 768), bf16),
            pltpu.VMEM((4, 8, 128), f32),
            pltpu.VMEM((4, 8, 128), f32),
            dma((2,)),
            dma((2, 3)), dma((2, 3)),
            dma((2, 4)), dma((2, 4)),
            dma((2, 3, 4)), dma((2, 3, 4)),
            dma((2, 4)), dma((2, 4)),
            dma((2, 4)), dma((2, 4)),
            dma((2, 8)), dma((2, 8)),
            dma((3, 8)), dma((3, 8)),
            dma((2, 4)), dma((2, 4)),
            dma((2, 3, 4)), dma((2, 3, 4)),
            dma((2, 4)), dma((2, 4)),
        ],
        compiler_params=pltpu.CompilerParams(
            collective_id=0, has_side_effects=True, vmem_limit_bytes=56 * 1024 * 1024
        ),
        cost_estimate=pl.CostEstimate(flops=4 * 2048 * 1536 * 768, bytes_accessed=4 << 20, transcendentals=2048 * 1536),
        name="dedup_scores",
    )(member_embed, sizes, order, ref_embed)
    return pl.pallas_call(
        hand_out,
        out_shape=(jax.ShapeDtypeStruct((1, 256), f32), jax.ShapeDtypeStruct((1, 256, 768), bf16)),
        in_specs=[vmem, vmem],
        out_specs=(vmem, vmem),
        cost_estimate=pl.CostEstimate(flops=0, bytes_accessed=1 << 20, transcendentals=0),
        name="hand_out",
    )(log_total, neighbour)


def solution(mesh):
    placed = (P("grp", "blk", None), P(), P("grp", "blk"), P(None, ("grp", "blk"), None))
    return jax.shard_map(
        per_device,
        mesh=mesh,
        in_specs=placed,
        out_specs=(P("grp", "blk"), P("grp", "blk", None)),
        check_vma=False,
    )
```

```python
import functools
import math

import jax
import jax.numpy as jnp
from jax import lax
from jax.experimental import pallas as pl
from jax.experimental.pallas import tpu as pltpu
from jax.sharding import PartitionSpec as P

SCALE = 32
MESH = pl.DeviceIdType.MESH
LOG2E = math.log2(math.e)
STEPS = (0, 2, 6, 1, 7, 3, 5, 4)


def unit_rows(values):
    mean_square = jnp.mean(values * values, axis=-1, keepdims=True)
    return (values * lax.rsqrt(mean_square + 1e-06)).astype(jnp.bfloat16)


def device(x, y, z, core):
    return ((x * 2 + y % 2) * 2 + core, (y // 2) * 8 + z)


def lanes_to_rows(tile):
    wide = jnp.concatenate([tile] * 8, axis=0)
    row = lax.broadcasted_iota(jnp.int32, (64, 128), 0)
    lane = lax.broadcasted_iota(jnp.int32, (64, 128), 1)
    return jnp.sum(jnp.where(row == lane, wide, 0.0), axis=1, keepdims=True)


def rows_to_lanes(column):
    row = lax.broadcasted_iota(jnp.int32, (64, 128), 0)
    lane = lax.broadcasted_iota(jnp.int32, (64, 128), 1)
    spread = jnp.where(row == lane % 64, jnp.broadcast_to(column, (64, 128)), 0.0)
    return jnp.broadcast_to(jnp.sum(spread, axis=0, keepdims=True), (8, 128))


def slot_position(delta):
    return delta + delta // 2 - 2 * (delta // 3)


def kernel(
    member_hbm, sizes_ref, order_ref, ref_hbm, log_ref, mean_ref,
    member_in, ref_in, home_rows, home_rank, hop_rows, hop_rank, ref_unit, query, rank, key_member, rank_partner, ref_other, key_ref,
    part_sum, part_total, lane_total, mix_send, mix_recv, tot_send, tot_recv, own_mix, own_tot,
    x_send, x_recv, xt_send, xt_recv, chain_rows, chain_total, done_rows, done_log, home_log,
    load_sem, s_q, r_q, s_a, r_a, s_x, r_x, s_c, r_c, s_y, r_y, s_z, r_z, s_ry, r_ry,
    s_m, r_m, s_t, r_t, s_h, r_h,
):
    g = lax.axis_index("grp")
    b = lax.axis_index("blk")
    x, y, z, core = g // 4, (b // 8) * 2 + (g // 2) % 2, b % 8, g % 2
    parity = y % 2
    other = 1 - core
    home_z = 2 * x + core
    work_x, work_core = z // 2, z % 2
    is_self = home_z == z
    stays = z % 2 == core
    work_group = (work_x * 2 + parity) * 2 + work_core

    z_steps = [(step + core * (8 - 2 * step)) % 8 for step in STEPS]
    x_steps = [step + core * (4 - 2 * step) for step in (2, 1, 3)]

    def source_z(position):
        return 2 * ((z // 2 + slot_position(position)) % 4) + core

    load_members = pltpu.make_async_copy(member_hbm.at[0], member_in, load_sem.at[0])
    load_refs = pltpu.make_async_copy(ref_hbm, ref_in, load_sem.at[1])
    load_members.start()
    load_refs.start()

    barrier = pltpu.get_barrier_semaphore()

    def greet(target):
        pl.semaphore_signal(barrier, inc=1, device_id=target, device_id_type=MESH)

    for step in (1, 2, 3):
        greet(device((x + step) % 4, y, z, core))
        greet(device(x, (y + step) % 4, z, core))
    for step in range(1, 8):
        greet(device(x, y, (z + step) % 8, core))
    greet(device(x, y, z, other))
    for position in range(4):
        from_z = source_z(position)

        @pl.when(jnp.logical_not(jnp.logical_and(stays, from_z == z)))
        def _():
            greet(device(x, y, from_z, z % 2))

    for quarter in range(4):

        @pl.when(jnp.logical_not(jnp.logical_and(is_self, x == quarter)))
        def _():
            greet(device(quarter, y, home_z, z % 2))

    load_members.wait()
    home_rows[...] = unit_rows(member_in[...])
    live_count = sizes_ref[g]
    slot = lax.broadcasted_iota(jnp.int32, (1, 256), 1) + b * 256
    ranks = jnp.where(slot < live_count, order_ref[...], 4096).astype(jnp.float32)
    for quarter in range(4):
        piece = ranks[:, 64 * quarter : 64 * quarter + 64]
        home_rank[quarter] = jnp.broadcast_to(jnp.concatenate([piece, piece], axis=1), (8, 128))

    load_refs.wait()
    for group in range(4):
        ref_unit[pl.ds(4 * group, 4)] = unit_rows(ref_in[pl.ds(4 * group, 4)])

    pl.semaphore_wait(barrier, 22 - is_self.astype(jnp.int32) - stays.astype(jnp.int32))

    sent = []

    def send(src, dst, send_sem, recv_sem, target):
        copy = pltpu.make_async_remote_copy(
            src_ref=src, dst_ref=dst, send_sem=send_sem, recv_sem=recv_sem, device_id=target, device_id_type=MESH
        )
        copy.start()
        sent.append(copy)
        return copy

    def landed(dst, sem):
        pltpu.make_async_copy(dst, dst, sem).wait()

    for i, step in enumerate(x_steps):
        to_x = (x + step) % 4
        target = device(to_x, y, z, core)
        quarter = pl.ds(pl.multiple_of(64 * to_x, 64), 64)
        send(home_rows.at[quarter], hop_rows.at[i], s_q.at[0, i], r_q.at[0, i], target)
        send(home_rank.at[to_x], hop_rank.at[i], s_q.at[1, i], r_q.at[1, i], target)

    row_owner = z % 2 * 4 + x
    first = []

    def to_row(i):
        from_x = (x + 4 - x_steps[i]) % 4 if i < 3 else x
        to_z = 2 * from_x + core
        here = slot_position((z // 2 - from_x + 4) % 4)
        if i < 3:
            rows, ranks = hop_rows.at[i], hop_rank.at[i]
            landed(rows, r_q.at[0, i])
            landed(ranks, r_q.at[1, i])
        else:
            rows, ranks = home_rows.at[pl.ds(pl.multiple_of(64 * x, 64), 64)], home_rank.at[x]
        mine = to_z == z
        for src, dst, kind in ((rows, query.at[here, row_owner], 0), (ranks, rank.at[here, row_owner], 1)):
            remote = pltpu.make_async_remote_copy(
                src_ref=src, dst_ref=dst, send_sem=s_a.at[kind, i], recv_sem=r_a.at[kind, here],
                device_id=device(x, y, to_z, z % 2), device_id_type=MESH,
            )
            local = pltpu.make_async_copy(src, dst, r_a.at[kind, here])
            first.append((mine, remote))

            @pl.when(mine)
            def _():
                local.start()

            @pl.when(jnp.logical_not(mine))
            def _():
                remote.start()

    def ref_index(to_z, side):
        return (to_z // 2) * 4 + side * 2 + to_z % 2

    key_ref[0, 0] = ref_unit[ref_index(z, parity)]
    ref_other[0] = ref_unit[ref_index(z, 1 - parity)]
    def send_refs(i):
        to_z = (z + 8 - z_steps[i]) % 8
        target = device(x, y, to_z, core)
        send(ref_unit.at[ref_index(to_z, parity)], key_ref.at[i, 0], s_z.at[0, i], r_z.at[0, i], target)
        send(ref_unit.at[ref_index(to_z, 1 - parity)], ref_other.at[i], s_z.at[1, i], r_z.at[1, i], target)

    opposite = device(x, (y + 2) % 4, z, core)
    above = device(x, (y + 1) % 4, z, core)
    below = device(x, (y + 3) % 4, z, core)

    def pass_refs(i):
        if i:
            landed(key_ref.at[i, 0], r_z.at[0, i])
            landed(ref_other.at[i], r_z.at[1, i])
        send(key_ref.at[i, 0], key_ref.at[i, 1], s_ry.at[0, i], r_ry.at[0, i], opposite)
        send(ref_other.at[i], key_ref.at[i, 2], s_ry.at[1, i], r_ry.at[1, i], above)
        send(ref_other.at[i], key_ref.at[i, 3], s_ry.at[2, i], r_ry.at[2, i], below)

    me = core * 4 + x

    def pass_queries(t):
        landed(query.at[t, me], r_a.at[0, t])
        landed(rank.at[t, me], r_a.at[1, t])
        for i, step in enumerate(x_steps):
            target = device((x + step) % 4, y, z, core)
            send(query.at[t, me], query.at[t, me], s_x.at[0, i, t], r_x.at[0, i, t], target)
            send(rank.at[t, me], rank.at[t, me], s_x.at[1, i, t], r_x.at[1, i, t], target)
        send(query.at[t, me], key_member.at[1, t], s_y.at[0, t], r_y.at[0, t], opposite)
        send(rank.at[t, me], rank_partner.at[t], s_y.at[1, t], r_y.at[1, t], opposite)
        key_member[0, t] = query[t, me]

    sibling = device(x, y, z, other)
    my_half, other_half = pl.ds(core * 4, 4), pl.ds(other * 4, 4)

    def share_queries(t):
        for i in (1, 2, 0):
            from_x = core * 4 + (x + 4 - x_steps[i]) % 4
            landed(query.at[t, from_x], r_x.at[0, i, t])
            landed(rank.at[t, from_x], r_x.at[1, i, t])
        send(query.at[t, my_half], query.at[t, my_half], s_c.at[0, t], r_c.at[0, t], sibling)
        send(rank.at[t, my_half], rank.at[t, my_half], s_c.at[1, t], r_c.at[1, t], sibling)

    low = lax.broadcasted_iota(jnp.int32, (8, 128), 1) < 64

    def queries_landed(t):
        landed(query.at[t, other_half], r_c.at[0, t])
        landed(rank.at[t, other_half], r_c.at[1, t])

    def members_landed():
        for t in range(4):
            landed(key_member.at[1, t], r_y.at[0, t])
            landed(rank_partner.at[t], r_y.at[1, t])

    def refs_landed(first, last):
        for i in range(first, last):
            for side in range(3):
                landed(key_ref.at[i, side + 1], r_ry.at[side, i])

    def weigh(rows, keys):
        logits = lax.dot_general(rows, keys, (((1,), (1,)), ((), ())), preferred_element_type=jnp.float32)
        return jnp.exp2(logits * (SCALE / 768 * LOG2E) - SCALE * LOG2E)

    def lane_sums(weight):
        return sum(weight[:, at : at + 128] for at in range(128, weight.shape[1], 128)) + weight[:, 0:128]

    begun = set()

    def add_up(t, weight, keys):
        mixed = jnp.dot(weight.astype(jnp.bfloat16), keys, preferred_element_type=jnp.float32).reshape(8, 64, 768)
        if t in begun:
            lane_total[t] += lane_sums(weight)
            part_sum[t] += mixed
        else:
            lane_total[t] = lane_sums(weight)
            part_sum[t] = mixed
            begun.add(t)

    def compute_members(t):
        key_rank = jnp.concatenate(
            [
                jnp.where(low, rank[0, me], rank[1, me]),
                jnp.where(low, rank[2, me], rank[3, me]),
                jnp.where(low, rank_partner[0], rank_partner[1]),
                jnp.where(low, rank_partner[2], rank_partner[3]),
            ],
            axis=1,
        )[0:1]
        row_rank = jnp.concatenate([lanes_to_rows(rank[t, owner]) for owner in range(8)], axis=0)
        keys = key_member[...].reshape(512, 768)
        weight = jnp.where(key_rank < row_rank, weigh(query[t].reshape(512, 768), keys), 0.0)
        add_up(t, weight, keys)

    def compute_refs(t, first, last):
        keys = key_ref[pl.ds(first, last - first)].reshape((last - first) * 128, 768)
        add_up(t, weigh(query[t].reshape(512, 768), keys), keys)

    def compute_last(t):
        keys = key_ref[pl.ds(4, 4)].reshape(512, 768)
        for side in (other, core):
            part = pl.ds(side * 4, 4)
            weight = weigh(query[t, part].reshape(256, 768), keys)
            sums = lane_total[t, pl.ds(pl.multiple_of(side * 256, 256), 256)] + lane_sums(weight)
            total = jnp.sum(sums, axis=1, keepdims=True)
            mixed = jnp.dot(weight.astype(jnp.bfloat16), keys, preferred_element_type=jnp.float32)
            mixed = part_sum[t, part] + mixed.reshape(4, 64, 768)
            if side is other:
                for owner in range(4):
                    tot_send[t, owner] = rows_to_lanes(total[64 * owner : 64 * owner + 64])
                mix_send[t] = mixed.astype(jnp.bfloat16)
                send(mix_send.at[t], mix_recv.at[t], s_m.at[0, t], r_m.at[0, t], sibling)
                send(tot_send.at[t], tot_recv.at[t], s_m.at[1, t], r_m.at[1, t], sibling)
            else:
                for owner in range(4):
                    part_total[t, side * 4 + owner] = rows_to_lanes(total[64 * owner : 64 * owner + 64])
                part_sum[t, part] = mixed

    def to_owner(t):
        landed(mix_recv.at[t], r_m.at[0, t])
        landed(tot_recv.at[t], r_m.at[1, t])
        mixed = part_sum[t, my_half] + mix_recv[t].astype(jnp.float32)
        total = part_total[t, my_half] + tot_recv[t]
        part_sum[t, my_half] = mixed
        part_total[t, my_half] = total
        x_send[t] = mixed.astype(jnp.bfloat16)
        xt_send[t] = total
        if t == 3:
            for i, step in enumerate(x_steps):
                send_part(t, i, x_send.at[t, (x + step) % 4], xt_send.at[t, (x + step) % 4], (x + step) % 4)
        else:
            far, near = (x + 2) % 4, (x + 4 - onward) % 4
            send_part(t, 0, x_send.at[t, far], xt_send.at[t, far], (x + onward) % 4)
            send_part(t, 1, x_send.at[t, near], xt_send.at[t, near], near)

    onward = x_steps[1]

    def send_part(t, i, rows, total, to_x):
        target = device(to_x, y, z, core)
        send(rows, x_recv.at[t, i], s_t.at[0, i, t], r_t.at[0, i, t], target)
        send(total, xt_recv.at[t, i], s_t.at[1, i, t], r_t.at[1, i, t], target)

    def part_landed(t, i):
        landed(x_recv.at[t, i], r_t.at[0, i, t])
        landed(xt_recv.at[t, i], r_t.at[1, i, t])

    def add_onward(t):
        part_landed(t, 0)
        to_x = (x + onward) % 4
        owner = core * 4 + to_x
        chain_rows[t] = (part_sum[t, owner] + x_recv[t, 0].astype(jnp.float32)).astype(jnp.bfloat16)
        chain_total[t] = part_total[t, owner] + xt_recv[t, 0]
        send_part(t, 2, chain_rows.at[t], chain_total.at[t], to_x)

    last = []

    def finish(t):
        mixed = part_sum[t, me]
        total = part_total[t, me]
        for i in (1, 2, 0) if t == 3 else (1, 2):
            part_landed(t, i)
            mixed = mixed + x_recv[t, i].astype(jnp.float32)
            total = total + xt_recv[t, i]
        from_z = source_z(t)
        start = (y // 2 * 8 + from_z) * 256 + 64 * x
        count = sizes_ref[work_group]
        slot_lane = lax.broadcasted_iota(jnp.int32, (8, 128), 1) % 64 + start
        divisor = jnp.where(slot_lane < count, total, 1.0)
        done_log[t] = jnp.where(slot_lane < count, SCALE + jnp.log(divisor), 0.0)
        slot_row = lax.broadcasted_iota(jnp.int32, (64, 1), 0) + start
        mean = jnp.where(slot_row < count, mixed / lanes_to_rows(divisor), 0.0)
        done_rows[t] = mean.astype(jnp.bfloat16)
        target = device(work_x, y, from_z, work_core)
        mine = jnp.logical_and(is_self, from_z == z)
        pairs = ((done_rows.at[t], mean_ref.at[0, pl.ds(pl.multiple_of(64 * x, 64), 64)], 0), (done_log.at[t], home_log.at[x], 1))
        for src, dst, kind in pairs:
            remote = pltpu.make_async_remote_copy(
                src_ref=src, dst_ref=dst, send_sem=s_h.at[kind, t], recv_sem=r_h.at[kind, x],
                device_id=target, device_id_type=MESH,
            )
            local = pltpu.make_async_copy(src, dst, r_h.at[kind, x])
            last.append((mine, remote))

            @pl.when(mine)
            def _():
                local.start()

            @pl.when(jnp.logical_not(mine))
            def _():
                remote.start()

    to_row(3)
    send_refs(1)
    send_refs(2)
    pass_refs(0)
    to_row(1)
    to_row(2)
    to_row(0)
    send_refs(3)
    send_refs(4)
    send_refs(5)
    send_refs(6)
    send_refs(7)
    pass_queries(0)
    pass_refs(1)
    pass_refs(2)
    pass_queries(1)
    pass_queries(2)
    pass_refs(3)
    pass_refs(4)
    share_queries(0)
    pass_queries(3)
    share_queries(1)
    share_queries(2)
    pass_refs(5)
    pass_refs(6)
    queries_landed(0)
    refs_landed(0, 4)
    compute_refs(0, 0, 4)
    queries_landed(1)
    compute_refs(1, 0, 4)
    share_queries(3)
    pass_refs(7)
    queries_landed(2)
    compute_refs(2, 0, 4)
    members_landed()
    compute_members(0)
    compute_members(1)
    queries_landed(3)
    compute_refs(3, 0, 4)
    refs_landed(4, 8)
    compute_last(0)
    compute_last(1)
    to_owner(0)
    compute_members(2)
    compute_last(2)
    to_owner(1)
    compute_members(3)
    compute_last(3)
    to_owner(2)
    to_owner(3)
    add_onward(0)
    add_onward(1)
    add_onward(2)
    finish(0)
    finish(1)
    finish(2)
    finish(3)

    for quarter in range(4):
        landed(mean_ref.at[0, pl.ds(64 * quarter, 64)], r_h.at[0, quarter])
        landed(home_log.at[quarter], r_h.at[1, quarter])
    log_ref[...] = jnp.concatenate(
        [jnp.where(low, home_log[0], home_log[1])[0:1], jnp.where(low, home_log[2], home_log[3])[0:1]], axis=1
    )
    for copy in sent:
        copy.wait_send()
    for mine, remote in first + last:

        @pl.when(jnp.logical_not(mine))
        def _():
            remote.wait_send()


def hand_out(log_in, mean_in, log_out, mean_out):
    log_out[...] = log_in[...]
    mean_out[...] = mean_in[...]


def per_device(member_embed, sizes, order, ref_embed):
    vmem = pl.BlockSpec(memory_space=pltpu.VMEM)
    anywhere = pl.BlockSpec(memory_space=pl.ANY)
    bf16, f32 = jnp.bfloat16, jnp.float32
    dma = pltpu.SemaphoreType.DMA
    log_total, neighbour = pl.pallas_call(
        kernel,
        out_shape=(jax.ShapeDtypeStruct((1, 256), f32), jax.ShapeDtypeStruct((1, 256, 768), bf16)),
        in_specs=[anywhere, pl.BlockSpec(memory_space=pltpu.SMEM), vmem, anywhere],
        out_specs=(vmem, vmem),
        scratch_shapes=[
            pltpu.VMEM((256, 768), f32),
            pltpu.VMEM((16, 32, 768), f32),
            pltpu.VMEM((256, 768), bf16),
            pltpu.VMEM((4, 8, 128), f32),
            pltpu.VMEM((3, 64, 768), bf16),
            pltpu.VMEM((3, 8, 128), f32),
            pltpu.VMEM((16, 32, 768), bf16),
            pltpu.VMEM((4, 8, 64, 768), bf16),
            pltpu.VMEM((4, 8, 8, 128), f32),
            pltpu.VMEM((2, 4, 64, 768), bf16),
            pltpu.VMEM((4, 8, 128), f32),
            pltpu.VMEM((8, 32, 768), bf16),
            pltpu.VMEM((8, 4, 32, 768), bf16),
            pltpu.VMEM((4, 8, 64, 768), f32),
            pltpu.VMEM((4, 8, 8, 128), f32),
            pltpu.VMEM((4, 512, 128), f32),
            pltpu.VMEM((4, 4, 64, 768), bf16),
            pltpu.VMEM((4, 4, 64, 768), bf16),
            pltpu.VMEM((4, 4, 8, 128), f32),
            pltpu.VMEM((4, 4, 8, 128), f32),
            pltpu.VMEM((8, 128), f32),
            pltpu.VMEM((8, 128), f32),
            pltpu.VMEM((4, 4, 64, 768), bf16),
            pltpu.VMEM((4, 3, 64, 768), bf16),
            pltpu.VMEM((4, 4, 8, 128), f32),
            pltpu.VMEM((4, 3, 8, 128), f32),
            pltpu.VMEM((3, 64, 768), bf16),
            pltpu.VMEM((3, 8, 128), f32),
            pltpu.VMEM((4, 64, 768), bf16),
            pltpu.VMEM((4, 8, 128), f32),
            pltpu.VMEM((4, 8, 128), f32),
            dma((2,)),
            dma((2, 3)), dma((2, 3)),
            dma((2, 4)), dma((2, 4)),
            dma((2, 3, 4)), dma((2, 3, 4)),
            dma((2, 4)), dma((2, 4)),
            dma((2, 4)), dma((2, 4)),
            dma((2, 8)), dma((2, 8)),
            dma((3, 8)), dma((3, 8)),
            dma((2, 4)), dma((2, 4)),
            dma((2, 3, 4)), dma((2, 3, 4)),
            dma((2, 4)), dma((2, 4)),
        ],
        compiler_params=pltpu.CompilerParams(
            collective_id=0, has_side_effects=True, vmem_limit_bytes=56 * 1024 * 1024
        ),
        cost_estimate=pl.CostEstimate(flops=4 * 2048 * 1536 * 768, bytes_accessed=4 << 20, transcendentals=2048 * 1536),
        name="dedup_scores",
    )(member_embed, sizes, order, ref_embed)
    return pl.pallas_call(
        hand_out,
        out_shape=(jax.ShapeDtypeStruct((1, 256), f32), jax.ShapeDtypeStruct((1, 256, 768), bf16)),
        in_specs=[vmem, vmem],
        out_specs=(vmem, vmem),
        cost_estimate=pl.CostEstimate(flops=0, bytes_accessed=1 << 20, transcendentals=0),
        name="hand_out",
    )(log_total, neighbour)


def solution(mesh):
    placed = (P("grp", "blk", None), P(), P("grp", "blk"), P(None, ("grp", "blk"), None))
    return jax.shard_map(
        per_device,
        mesh=mesh,
        in_specs=placed,
        out_specs=(P("grp", "blk"), P("grp", "blk", None)),
        check_vma=False,
    )
```

```python
import functools
import math

import jax
import jax.numpy as jnp
from jax import lax
from jax.experimental import pallas as pl
from jax.experimental.pallas import tpu as pltpu
from jax.sharding import PartitionSpec as P

SCALE = 32
MESH = pl.DeviceIdType.MESH
LOG2E = math.log2(math.e)
STEPS = (0, 2, 6, 1, 7, 3, 5, 4)


def unit_rows(values):
    mean_square = jnp.mean(values * values, axis=-1, keepdims=True)
    return (values * lax.rsqrt(mean_square + 1e-06)).astype(jnp.bfloat16)


def device(x, y, z, core):
    return ((x * 2 + y % 2) * 2 + core, (y // 2) * 8 + z)


def lanes_to_rows(tile):
    wide = jnp.concatenate([tile] * 8, axis=0)
    row = lax.broadcasted_iota(jnp.int32, (64, 128), 0)
    lane = lax.broadcasted_iota(jnp.int32, (64, 128), 1)
    return jnp.sum(jnp.where(row == lane, wide, 0.0), axis=1, keepdims=True)


def rows_to_lanes(column):
    row = lax.broadcasted_iota(jnp.int32, (64, 128), 0)
    lane = lax.broadcasted_iota(jnp.int32, (64, 128), 1)
    spread = jnp.where(row == lane % 64, jnp.broadcast_to(column, (64, 128)), 0.0)
    return jnp.broadcast_to(jnp.sum(spread, axis=0, keepdims=True), (8, 128))


def slot_position(delta):
    return delta + delta // 2 - 2 * (delta // 3)


def kernel(
    member_hbm, sizes_ref, order_ref, ref_hbm, log_ref, mean_ref,
    member_in, ref_in, home_rows, home_rank, hop_rows, hop_rank, ref_unit, query, rank, key_member, rank_partner, ref_other, key_ref,
    part_sum, part_total, lane_total, mix_send, mix_recv, tot_send, tot_recv, own_mix, own_tot,
    x_send, x_recv, xt_send, xt_recv, chain_rows, chain_total, done_rows, done_log, home_log,
    load_sem, s_q, r_q, s_a, r_a, s_x, r_x, s_c, r_c, s_y, r_y, s_z, r_z, s_ry, r_ry,
    s_m, r_m, s_t, r_t, s_h, r_h,
):
    g = lax.axis_index("grp")
    b = lax.axis_index("blk")
    x, y, z, core = g // 4, (b // 8) * 2 + (g // 2) % 2, b % 8, g % 2
    parity = y % 2
    other = 1 - core
    home_z = 2 * x + core
    work_x, work_core = z // 2, z % 2
    is_self = home_z == z
    stays = z % 2 == core
    work_group = (work_x * 2 + parity) * 2 + work_core

    z_steps = [(step + core * (8 - 2 * step)) % 8 for step in STEPS]
    x_steps = [step + core * (4 - 2 * step) for step in (2, 1, 3)]

    def source_z(position):
        return 2 * ((z // 2 + slot_position(position)) % 4) + core

    load_members = pltpu.make_async_copy(member_hbm.at[0], member_in, load_sem.at[0])
    load_refs = pltpu.make_async_copy(ref_hbm, ref_in, load_sem.at[1])
    load_members.start()
    load_refs.start()

    barrier = pltpu.get_barrier_semaphore()

    def greet(target):
        pl.semaphore_signal(barrier, inc=1, device_id=target, device_id_type=MESH)

    for step in (1, 2, 3):
        greet(device((x + step) % 4, y, z, core))
        greet(device(x, (y + step) % 4, z, core))
    for step in range(1, 8):
        greet(device(x, y, (z + step) % 8, core))
    greet(device(x, y, z, other))
    for position in range(4):
        from_z = source_z(position)

        @pl.when(jnp.logical_not(jnp.logical_and(stays, from_z == z)))
        def _():
            greet(device(x, y, from_z, z % 2))

    for quarter in range(4):

        @pl.when(jnp.logical_not(jnp.logical_and(is_self, x == quarter)))
        def _():
            greet(device(quarter, y, home_z, z % 2))

    load_members.wait()
    home_rows[...] = unit_rows(member_in[...])
    live_count = sizes_ref[g]
    slot = lax.broadcasted_iota(jnp.int32, (1, 256), 1) + b * 256
    ranks = jnp.where(slot < live_count, order_ref[...], 4096).astype(jnp.float32)
    for quarter in range(4):
        piece = ranks[:, 64 * quarter : 64 * quarter + 64]
        home_rank[quarter] = jnp.broadcast_to(jnp.concatenate([piece, piece], axis=1), (8, 128))

    load_refs.wait()
    for group in range(4):
        ref_unit[pl.ds(4 * group, 4)] = unit_rows(ref_in[pl.ds(4 * group, 4)])

    pl.semaphore_wait(barrier, 22 - is_self.astype(jnp.int32) - stays.astype(jnp.int32))

    sent = []

    def send(src, dst, send_sem, recv_sem, target):
        copy = pltpu.make_async_remote_copy(
            src_ref=src, dst_ref=dst, send_sem=send_sem, recv_sem=recv_sem, device_id=target, device_id_type=MESH
        )
        copy.start()
        sent.append(copy)
        return copy

    def landed(dst, sem):
        pltpu.make_async_copy(dst, dst, sem).wait()

    for i, step in enumerate(x_steps):
        to_x = (x + step) % 4
        target = device(to_x, y, z, core)
        quarter = pl.ds(pl.multiple_of(64 * to_x, 64), 64)
        send(home_rows.at[quarter], hop_rows.at[i], s_q.at[0, i], r_q.at[0, i], target)
        send(home_rank.at[to_x], hop_rank.at[i], s_q.at[1, i], r_q.at[1, i], target)

    row_owner = z % 2 * 4 + x
    first = []

    def to_row(i):
        from_x = (x + 4 - x_steps[i]) % 4 if i < 3 else x
        to_z = 2 * from_x + core
        here = slot_position((z // 2 - from_x + 4) % 4)
        if i < 3:
            rows, ranks = hop_rows.at[i], hop_rank.at[i]
            landed(rows, r_q.at[0, i])
            landed(ranks, r_q.at[1, i])
        else:
            rows, ranks = home_rows.at[pl.ds(pl.multiple_of(64 * x, 64), 64)], home_rank.at[x]
        mine = to_z == z
        for src, dst, kind in ((rows, query.at[here, row_owner], 0), (ranks, rank.at[here, row_owner], 1)):
            remote = pltpu.make_async_remote_copy(
                src_ref=src, dst_ref=dst, send_sem=s_a.at[kind, i], recv_sem=r_a.at[kind, here],
                device_id=device(x, y, to_z, z % 2), device_id_type=MESH,
            )
            local = pltpu.make_async_copy(src, dst, r_a.at[kind, here])
            first.append((mine, remote))

            @pl.when(mine)
            def _():
                local.start()

            @pl.when(jnp.logical_not(mine))
            def _():
                remote.start()

    def ref_index(to_z, side):
        return (to_z // 2) * 4 + side * 2 + to_z % 2

    key_ref[0, 0] = ref_unit[ref_index(z, parity)]
    ref_other[0] = ref_unit[ref_index(z, 1 - parity)]
    def send_refs(i):
        to_z = (z + 8 - z_steps[i]) % 8
        target = device(x, y, to_z, core)
        send(ref_unit.at[ref_index(to_z, parity)], key_ref.at[i, 0], s_z.at[0, i], r_z.at[0, i], target)
        send(ref_unit.at[ref_index(to_z, 1 - parity)], ref_other.at[i], s_z.at[1, i], r_z.at[1, i], target)

    opposite = device(x, (y + 2) % 4, z, core)
    above = device(x, (y + 1) % 4, z, core)
    below = device(x, (y + 3) % 4, z, core)

    def pass_refs(i):
        if i:
            landed(key_ref.at[i, 0], r_z.at[0, i])
            landed(ref_other.at[i], r_z.at[1, i])
        send(key_ref.at[i, 0], key_ref.at[i, 1], s_ry.at[0, i], r_ry.at[0, i], opposite)
        send(ref_other.at[i], key_ref.at[i, 2], s_ry.at[1, i], r_ry.at[1, i], above)
        send(ref_other.at[i], key_ref.at[i, 3], s_ry.at[2, i], r_ry.at[2, i], below)

    me = core * 4 + x

    def pass_queries(t):
        landed(query.at[t, me], r_a.at[0, t])
        landed(rank.at[t, me], r_a.at[1, t])
        for i, step in enumerate(x_steps):
            target = device((x + step) % 4, y, z, core)
            send(query.at[t, me], query.at[t, me], s_x.at[0, i, t], r_x.at[0, i, t], target)
            send(rank.at[t, me], rank.at[t, me], s_x.at[1, i, t], r_x.at[1, i, t], target)
        send(query.at[t, me], key_member.at[1, t], s_y.at[0, t], r_y.at[0, t], opposite)
        send(rank.at[t, me], rank_partner.at[t], s_y.at[1, t], r_y.at[1, t], opposite)
        key_member[0, t] = query[t, me]

    sibling = device(x, y, z, other)
    my_half, other_half = pl.ds(core * 4, 4), pl.ds(other * 4, 4)

    def share_queries(t):
        for i in (1, 2, 0):
            from_x = core * 4 + (x + 4 - x_steps[i]) % 4
            landed(query.at[t, from_x], r_x.at[0, i, t])
            landed(rank.at[t, from_x], r_x.at[1, i, t])
        send(query.at[t, my_half], query.at[t, my_half], s_c.at[0, t], r_c.at[0, t], sibling)
        send(rank.at[t, my_half], rank.at[t, my_half], s_c.at[1, t], r_c.at[1, t], sibling)

    low = lax.broadcasted_iota(jnp.int32, (8, 128), 1) < 64

    def queries_landed(t):
        landed(query.at[t, other_half], r_c.at[0, t])
        landed(rank.at[t, other_half], r_c.at[1, t])

    def members_landed():
        for t in range(4):
            landed(key_member.at[1, t], r_y.at[0, t])
            landed(rank_partner.at[t], r_y.at[1, t])

    def refs_landed(first, last):
        for i in range(first, last):
            for side in range(3):
                landed(key_ref.at[i, side + 1], r_ry.at[side, i])

    def weigh(rows, keys):
        logits = lax.dot_general(rows, keys, (((1,), (1,)), ((), ())), preferred_element_type=jnp.float32)
        return jnp.exp2(logits * (SCALE / 768 * LOG2E) - SCALE * LOG2E)

    def lane_sums(weight):
        return sum(weight[:, at : at + 128] for at in range(128, weight.shape[1], 128)) + weight[:, 0:128]

    begun = set()

    def add_up(t, weight, keys):
        mixed = jnp.dot(weight.astype(jnp.bfloat16), keys, preferred_element_type=jnp.float32).reshape(8, 64, 768)
        if t in begun:
            lane_total[t] += lane_sums(weight)
            part_sum[t] += mixed
        else:
            lane_total[t] = lane_sums(weight)
            part_sum[t] = mixed
            begun.add(t)

    def compute_members(t):
        key_rank = jnp.concatenate(
            [
                jnp.where(low, rank[0, me], rank[1, me]),
                jnp.where(low, rank[2, me], rank[3, me]),
                jnp.where(low, rank_partner[0], rank_partner[1]),
                jnp.where(low, rank_partner[2], rank_partner[3]),
            ],
            axis=1,
        )[0:1]
        row_rank = jnp.concatenate([lanes_to_rows(rank[t, owner]) for owner in range(8)], axis=0)
        keys = key_member[...].reshape(512, 768)
        weight = jnp.where(key_rank < row_rank, weigh(query[t].reshape(512, 768), keys), 0.0)
        add_up(t, weight, keys)

    def compute_refs(t, first, last):
        keys = key_ref[pl.ds(first, last - first)].reshape((last - first) * 128, 768)
        add_up(t, weigh(query[t].reshape(512, 768), keys), keys)

    def compute_last(t):
        keys = key_ref[pl.ds(4, 4)].reshape(512, 768)
        for side in (other, core):
            part = pl.ds(side * 4, 4)
            weight = weigh(query[t, part].reshape(256, 768), keys)
            sums = lane_total[t, pl.ds(pl.multiple_of(side * 256, 256), 256)] + lane_sums(weight)
            total = jnp.sum(sums, axis=1, keepdims=True)
            mixed = jnp.dot(weight.astype(jnp.bfloat16), keys, preferred_element_type=jnp.float32)
            mixed = part_sum[t, part] + mixed.reshape(4, 64, 768)
            if side is other:
                for owner in range(4):
                    tot_send[t, owner] = rows_to_lanes(total[64 * owner : 64 * owner + 64])
                mix_send[t] = mixed.astype(jnp.bfloat16)
                send(mix_send.at[t], mix_recv.at[t], s_m.at[0, t], r_m.at[0, t], sibling)
                send(tot_send.at[t], tot_recv.at[t], s_m.at[1, t], r_m.at[1, t], sibling)
            else:
                for owner in range(4):
                    part_total[t, side * 4 + owner] = rows_to_lanes(total[64 * owner : 64 * owner + 64])
                part_sum[t, part] = mixed

    def to_owner(t):
        landed(mix_recv.at[t], r_m.at[0, t])
        landed(tot_recv.at[t], r_m.at[1, t])
        mixed = part_sum[t, my_half] + mix_recv[t].astype(jnp.float32)
        total = part_total[t, my_half] + tot_recv[t]
        part_sum[t, my_half] = mixed
        part_total[t, my_half] = total
        x_send[t] = mixed.astype(jnp.bfloat16)
        xt_send[t] = total
        if t == 3:
            for i, step in enumerate(x_steps):
                send_part(t, i, x_send.at[t, (x + step) % 4], xt_send.at[t, (x + step) % 4], (x + step) % 4)
        else:
            far, near = (x + 2) % 4, (x + 4 - onward) % 4
            send_part(t, 0, x_send.at[t, far], xt_send.at[t, far], (x + onward) % 4)
            send_part(t, 1, x_send.at[t, near], xt_send.at[t, near], near)

    onward = x_steps[1]

    def send_part(t, i, rows, total, to_x):
        target = device(to_x, y, z, core)
        send(rows, x_recv.at[t, i], s_t.at[0, i, t], r_t.at[0, i, t], target)
        send(total, xt_recv.at[t, i], s_t.at[1, i, t], r_t.at[1, i, t], target)

    def part_landed(t, i):
        landed(x_recv.at[t, i], r_t.at[0, i, t])
        landed(xt_recv.at[t, i], r_t.at[1, i, t])

    def add_onward(t):
        part_landed(t, 0)
        to_x = (x + onward) % 4
        owner = core * 4 + to_x
        chain_rows[t] = (part_sum[t, owner] + x_recv[t, 0].astype(jnp.float32)).astype(jnp.bfloat16)
        chain_total[t] = part_total[t, owner] + xt_recv[t, 0]
        send_part(t, 2, chain_rows.at[t], chain_total.at[t], to_x)

    last = []

    def finish(t):
        mixed = part_sum[t, me]
        total = part_total[t, me]
        for i in (1, 2, 0) if t == 3 else (1, 2):
            part_landed(t, i)
            mixed = mixed + x_recv[t, i].astype(jnp.float32)
            total = total + xt_recv[t, i]
        from_z = source_z(t)
        start = (y // 2 * 8 + from_z) * 256 + 64 * x
        count = sizes_ref[work_group]
        slot_lane = lax.broadcasted_iota(jnp.int32, (8, 128), 1) % 64 + start
        divisor = jnp.where(slot_lane < count, total, 1.0)
        done_log[t] = jnp.where(slot_lane < count, SCALE + jnp.log(divisor), 0.0)
        slot_row = lax.broadcasted_iota(jnp.int32, (64, 1), 0) + start
        mean = jnp.where(slot_row < count, mixed / lanes_to_rows(divisor), 0.0)
        done_rows[t] = mean.astype(jnp.bfloat16)
        target = device(work_x, y, from_z, work_core)
        mine = jnp.logical_and(is_self, from_z == z)
        pairs = ((done_rows.at[t], mean_ref.at[0, pl.ds(pl.multiple_of(64 * x, 64), 64)], 0), (done_log.at[t], home_log.at[x], 1))
        for src, dst, kind in pairs:
            remote = pltpu.make_async_remote_copy(
                src_ref=src, dst_ref=dst, send_sem=s_h.at[kind, t], recv_sem=r_h.at[kind, x],
                device_id=target, device_id_type=MESH,
            )
            local = pltpu.make_async_copy(src, dst, r_h.at[kind, x])
            last.append((mine, remote))

            @pl.when(mine)
            def _():
                local.start()

            @pl.when(jnp.logical_not(mine))
            def _():
                remote.start()

    to_row(3)
    send_refs(1)
    send_refs(2)
    pass_refs(0)
    to_row(1)
    to_row(2)
    to_row(0)
    send_refs(3)
    send_refs(4)
    send_refs(5)
    send_refs(6)
    send_refs(7)
    pass_queries(0)
    pass_refs(1)
    pass_refs(2)
    pass_queries(1)
    pass_queries(2)
    pass_refs(3)
    pass_refs(4)
    share_queries(0)
    pass_queries(3)
    share_queries(1)
    share_queries(2)
    pass_refs(5)
    pass_refs(6)
    queries_landed(0)
    refs_landed(0, 4)
    compute_refs(0, 0, 4)
    queries_landed(1)
    compute_refs(1, 0, 4)
    share_queries(3)
    pass_refs(7)
    queries_landed(2)
    compute_refs(2, 0, 4)
    members_landed()
    compute_members(0)
    compute_members(1)
    refs_landed(4, 8)
    compute_last(0)
    compute_last(1)
    to_owner(0)
    compute_members(2)
    compute_last(2)
    to_owner(1)
    queries_landed(3)
    compute_refs(3, 0, 4)
    compute_members(3)
    compute_last(3)
    to_owner(2)
    to_owner(3)
    add_onward(0)
    add_onward(1)
    add_onward(2)
    finish(0)
    finish(1)
    finish(2)
    finish(3)

    for quarter in range(4):
        landed(mean_ref.at[0, pl.ds(64 * quarter, 64)], r_h.at[0, quarter])
        landed(home_log.at[quarter], r_h.at[1, quarter])
    log_ref[...] = jnp.concatenate(
        [jnp.where(low, home_log[0], home_log[1])[0:1], jnp.where(low, home_log[2], home_log[3])[0:1]], axis=1
    )
    for copy in sent:
        copy.wait_send()
    for mine, remote in first + last:

        @pl.when(jnp.logical_not(mine))
        def _():
            remote.wait_send()


def hand_out(log_in, mean_in, log_out, mean_out):
    log_out[...] = log_in[...]
    mean_out[...] = mean_in[...]


def per_device(member_embed, sizes, order, ref_embed):
    vmem = pl.BlockSpec(memory_space=pltpu.VMEM)
    anywhere = pl.BlockSpec(memory_space=pl.ANY)
    bf16, f32 = jnp.bfloat16, jnp.float32
    dma = pltpu.SemaphoreType.DMA
    log_total, neighbour = pl.pallas_call(
        kernel,
        out_shape=(jax.ShapeDtypeStruct((1, 256), f32), jax.ShapeDtypeStruct((1, 256, 768), bf16)),
        in_specs=[anywhere, pl.BlockSpec(memory_space=pltpu.SMEM), vmem, anywhere],
        out_specs=(vmem, vmem),
        scratch_shapes=[
            pltpu.VMEM((256, 768), f32),
            pltpu.VMEM((16, 32, 768), f32),
            pltpu.VMEM((256, 768), bf16),
            pltpu.VMEM((4, 8, 128), f32),
            pltpu.VMEM((3, 64, 768), bf16),
            pltpu.VMEM((3, 8, 128), f32),
            pltpu.VMEM((16, 32, 768), bf16),
            pltpu.VMEM((4, 8, 64, 768), bf16),
            pltpu.VMEM((4, 8, 8, 128), f32),
            pltpu.VMEM((2, 4, 64, 768), bf16),
            pltpu.VMEM((4, 8, 128), f32),
            pltpu.VMEM((8, 32, 768), bf16),
            pltpu.VMEM((8, 4, 32, 768), bf16),
            pltpu.VMEM((4, 8, 64, 768), f32),
            pltpu.VMEM((4, 8, 8, 128), f32),
            pltpu.VMEM((4, 512, 128), f32),
            pltpu.VMEM((4, 4, 64, 768), bf16),
            pltpu.VMEM((4, 4, 64, 768), bf16),
            pltpu.VMEM((4, 4, 8, 128), f32),
            pltpu.VMEM((4, 4, 8, 128), f32),
            pltpu.VMEM((8, 128), f32),
            pltpu.VMEM((8, 128), f32),
            pltpu.VMEM((4, 4, 64, 768), bf16),
            pltpu.VMEM((4, 3, 64, 768), bf16),
            pltpu.VMEM((4, 4, 8, 128), f32),
            pltpu.VMEM((4, 3, 8, 128), f32),
            pltpu.VMEM((3, 64, 768), bf16),
            pltpu.VMEM((3, 8, 128), f32),
            pltpu.VMEM((4, 64, 768), bf16),
            pltpu.VMEM((4, 8, 128), f32),
            pltpu.VMEM((4, 8, 128), f32),
            dma((2,)),
            dma((2, 3)), dma((2, 3)),
            dma((2, 4)), dma((2, 4)),
            dma((2, 3, 4)), dma((2, 3, 4)),
            dma((2, 4)), dma((2, 4)),
            dma((2, 4)), dma((2, 4)),
            dma((2, 8)), dma((2, 8)),
            dma((3, 8)), dma((3, 8)),
            dma((2, 4)), dma((2, 4)),
            dma((2, 3, 4)), dma((2, 3, 4)),
            dma((2, 4)), dma((2, 4)),
        ],
        compiler_params=pltpu.CompilerParams(
            collective_id=0, has_side_effects=True, vmem_limit_bytes=56 * 1024 * 1024
        ),
        cost_estimate=pl.CostEstimate(flops=4 * 2048 * 1536 * 768, bytes_accessed=4 << 20, transcendentals=2048 * 1536),
        name="dedup_scores",
    )(member_embed, sizes, order, ref_embed)
    return pl.pallas_call(
        hand_out,
        out_shape=(jax.ShapeDtypeStruct((1, 256), f32), jax.ShapeDtypeStruct((1, 256, 768), bf16)),
        in_specs=[vmem, vmem],
        out_specs=(vmem, vmem),
        cost_estimate=pl.CostEstimate(flops=0, bytes_accessed=1 << 20, transcendentals=0),
        name="hand_out",
    )(log_total, neighbour)


def solution(mesh):
    placed = (P("grp", "blk", None), P(), P("grp", "blk"), P(None, ("grp", "blk"), None))
    return jax.shard_map(
        per_device,
        mesh=mesh,
        in_specs=placed,
        out_specs=(P("grp", "blk"), P("grp", "blk", None)),
        check_vma=False,
    )
```
